32 devices in a mesh: cell: 8 (over z, y), view: 4 (over x, core).
Axes of the slice: x: 2, y: 2, z: 4, core: 2. Of those that a mesh axis runs over, the one named last changes fastest.
Arguments:
- gaussians: float32 [128, 9, 256], P('cell'), as said below
- seg_count: int32 [4, 8], P('view', 'cell'), may hold values from 1 to 3, as said below
- seg_block: int32 [4, 8, 3], P('view', 'cell'), may hold values from 0 to 127, as said below
- ray_count: int32 [4, 8], P('view', 'cell'), may hold values from 576 to 2304
- camera_shift: float32 [4, 2], P('view'), may hold values from -6 to 6
- target: float32 [4, 8, 3, 2304], P('view', 'cell'), may hold values from 0 to 1
Outputs:
- image: float32 [4, 8, 3, 2304], P('view', 'cell')
- gauss_grad: float32 [128, 9, 256], P('cell')
The draws below stay inside these ranges and needn't reach their ends.
Inputs may be any that keep to these rules, and one draw needn't show every extreme that they name: `gaussians`: each column of a block is one Gaussian: a mean, the entries a, b, c of a positive definite inverse covariance, an opacity in (0, 1), three colours. `seg_count`: tiles 2m and 2m + 1 of a view hold 4 segments together; in every view some tile holds 3. Segment k of tile t uses a block stored in cell seg_block // 16, which is t + e modulo 8 for some e from -2 to 2; entries at k >= seg_count are not used.
All inputs are finite; a program needn't handle non-finite values.
Results may differ from the reference program's by a relative error of at most 0.0003.
Values sent between devices are 32-bit elements; how exact they have to be, the bound alone decides.
A program may use at most 64 MiB of HBM per device.

```python
import math
from functools import partial
import jax
import jax.numpy as jnp
from jax import lax

TILE = 48
PIX = 2304
GB = 256
SEG_MAX = 3
REACH = 2
BLOCKS_DEV = 16
BLOCKS = 128
TILES = 8
VIEWS = 4


def draw_gaussians(key, part):
    subkeys = jax.random.split(key, 7)
    grid_shape = (BLOCKS, GB)
    sigma_low, sigma_high, opacity_low, opacity_high, colour_low = (TILE / 16.0, TILE / 3.0, 0.004, 0.04, 0.0)
    mean_x = jax.random.uniform(subkeys[0], grid_shape, jnp.float32, -0.6 * TILE, 0.6 * TILE)
    mean_y = jax.random.uniform(subkeys[1], grid_shape, jnp.float32, -0.6 * TILE, 0.6 * TILE)
    sigma_x = jnp.exp(jax.random.uniform(subkeys[2], grid_shape, jnp.float32, math.log(sigma_low), math.log(sigma_high)))
    sigma_y = jnp.exp(jax.random.uniform(subkeys[3], grid_shape, jnp.float32, math.log(sigma_low), math.log(sigma_high)))
    correl = jax.random.uniform(subkeys[4], grid_shape, jnp.float32, -0.6, 0.6)
    shrink = 1.0 - correl * correl
    conic_a = 1.0 / (sigma_x * sigma_x * shrink)
    conic_c = 1.0 / (sigma_y * sigma_y * shrink)
    conic_b = -correl / (sigma_x * sigma_y * shrink)
    opacity = jnp.exp(jax.random.uniform(subkeys[5], grid_shape, jnp.float32, math.log(opacity_low), math.log(opacity_high)))
    colours = jax.random.uniform(subkeys[6], (3, BLOCKS, GB), jnp.float32, colour_low, 1.0)
    stacked = jnp.stack([mean_x, mean_y, conic_a, conic_b, conic_c, opacity, colours[0], colours[1], colours[2]], axis=1)
    return stacked.astype(jnp.float32)


def draw_seg_count(key, part):
    subkeys = jax.random.split(key, 3)
    pair_total = TILES // 2
    even_count = jax.random.randint(subkeys[0], (VIEWS, pair_total), 1, SEG_MAX + 1)
    chosen = jax.random.randint(subkeys[1], (VIEWS,), 0, pair_total)
    full_side = jax.random.randint(subkeys[2], (VIEWS,), 0, 2)
    full_value = jnp.where(full_side == 0, SEG_MAX, 1)
    even_count = jnp.where(jnp.arange(pair_total)[None, :] == chosen[:, None], full_value[:, None], even_count)
    odd_count = SEG_MAX + 1 - even_count
    return jnp.stack([even_count, odd_count], axis=-1).reshape(VIEWS, TILES).astype(jnp.int32)


def draw_seg_block(key, part):
    subkeys = jax.random.split(key, 2)
    grid_shape = (VIEWS, TILES, SEG_MAX)
    offset = jax.random.randint(subkeys[0], grid_shape, -REACH, REACH + 1)
    local_block = jax.random.randint(subkeys[1], grid_shape, 0, BLOCKS_DEV)
    tile_ids = jnp.arange(TILES)[None, :, None]
    home_cell = (tile_ids + offset) % TILES
    return (home_cell * BLOCKS_DEV + local_block).astype(jnp.int32)


def touch_ends(drawn, stream_key, smallest, high):
    index_at = [jax.random.randint(jax.random.fold_in(stream_key, axis), (), 0, length) for axis, length in enumerate(drawn.shape)]
    widest = drawn.shape.index(max(drawn.shape))
    beside = index_at[:widest] + [(index_at[widest] + 1) % drawn.shape[widest]] + index_at[widest + 1:]
    return drawn.at[tuple(index_at)].set(smallest).at[tuple(beside)].set(high)


def block_scale(key, extent, cuts, smallest, largest):
    loudness = 1.0
    for position, shards_of in cuts:
        heights = jax.random.uniform(jax.random.fold_in(jax.random.fold_in(key, 6), position), (shards_of,), jnp.float32, smallest / len(cuts), largest / len(cuts))
        loudness = loudness * jnp.repeat(jnp.exp(heights), extent[position] // shards_of).reshape((-1,) + (1,) * (len(extent) - 1 - position))
    return loudness


def setup_inputs(seed: int = 0) -> dict:
    streams_of = jax.random.split(jax.random.key(seed), 7)
    gaussians = draw_gaussians(jax.random.fold_in(streams_of[6], 71), 0)
    seg_count = draw_seg_count(jax.random.fold_in(streams_of[6], 71), 0)
    seg_block = draw_seg_block(jax.random.fold_in(streams_of[6], 71), 0)
    ray_count = touch_ends(jax.random.randint(streams_of[3], (VIEWS, TILES), PIX // 4, PIX + 1), jax.random.fold_in(streams_of[3], 1), PIX // 4, PIX).astype(jnp.int32)
    camera_shift = jnp.clip(jax.random.uniform(streams_of[4], (VIEWS, 2), jnp.float32, -6.0, 6.0) * block_scale(streams_of[4], (VIEWS, 2), ((0, 4),), -0.4, 0.0), -6.0, 6.0)
    target = jnp.clip(1.0 * jax.random.uniform(streams_of[5], (VIEWS, TILES, 3, PIX), jnp.float32) ** block_scale(streams_of[5], (VIEWS, TILES, 3, PIX), ((0, 4), (1, 8)), -0.2, 0.2), 0.0, 1.0)
    return {"gaussians": gaussians, "seg_count": seg_count, "seg_block": seg_block, "ray_count": ray_count, "camera_shift": camera_shift, "target": target}


precise = lax.Precision.HIGHEST


def pixel_frame(shift):
    pixel_ids = jnp.arange(PIX)
    centre = (TILE - 1) / 2.0
    pix_x = (pixel_ids % TILE).astype(jnp.float32) - centre - shift[0]
    pix_y = (pixel_ids // TILE).astype(jnp.float32) - centre - shift[1]
    return pix_x, pix_y


def splat(params, pix_x, pix_y):
    delta_x = pix_x[None, :] - params[0][:, None]
    delta_y = pix_y[None, :] - params[1][:, None]
    quad_form = params[2][:, None] * delta_x * delta_x + 2.0 * params[3][:, None] * delta_x * delta_y + params[4][:, None] * delta_y * delta_y
    alphas = params[5][:, None] * jnp.exp(-0.5 * quad_form)
    return alphas, jnp.log1p(-alphas)


def forward_task(params, pix_x, pix_y):
    alphas, log_trans = splat(params, pix_x, pix_y)
    prefix = jnp.cumsum(log_trans, axis=0) - log_trans
    weights = alphas * jnp.exp(prefix)
    colour = jnp.dot(params[6:9], weights, precision=precise, preferred_element_type=jnp.float32)
    totals = jnp.sum(log_trans, axis=0)
    return jnp.concatenate([colour, totals[None, :]], axis=0)


def gradient_rows(params, pix_x, pix_y, weighted, weights, weight_cot):
    features = jnp.stack([jnp.ones_like(pix_x), pix_x, pix_y, pix_x * pix_x, pix_x * pix_y, pix_y * pix_y])
    moments = lax.dot_general(features, weighted, (((1,), (1,)), ((), ())), precision=precise, preferred_element_type=jnp.float32)
    colour_grad = lax.dot_general(weight_cot, weights, (((1,), (1,)), ((), ())), precision=precise, preferred_element_type=jnp.float32)
    mean_x, mean_y, conic_a, conic_b, conic_c, opacity = params[0], params[1], params[2], params[3], params[4], params[5]
    moment_zero = moments[0]
    along_x = moments[1] - mean_x * moment_zero
    along_y = moments[2] - mean_y * moment_zero
    square_x = moments[3] - 2.0 * mean_x * moments[1] + mean_x * mean_x * moment_zero
    cross_xy = moments[4] - mean_x * moments[2] - mean_y * moments[1] + mean_x * mean_y * moment_zero
    square_y = moments[5] - 2.0 * mean_y * moments[2] + mean_y * mean_y * moment_zero
    grad_rows = jnp.stack([conic_a * along_x + conic_b * along_y, conic_b * along_x + conic_c * along_y, -0.5 * square_x, -cross_xy, -0.5 * square_y, moment_zero / opacity])
    return jnp.concatenate([grad_rows, colour_grad], axis=0)


def backward_task(params, cotangent, pix_x, pix_y):
    alphas, log_trans = splat(params, pix_x, pix_y)
    transmit = jnp.exp(jnp.cumsum(log_trans, axis=0) - log_trans)
    weights = alphas * transmit
    weight_cot = cotangent[:3]
    shaded = lax.dot_general(params[6:9], weight_cot, (((0,), (0,)), ((), ())), precision=precise, preferred_element_type=jnp.float32)
    products = weights * shaded
    later_sum = jnp.sum(products, axis=0, keepdims=True) - jnp.cumsum(products, axis=0)
    dalpha = transmit * shaded - (later_sum + cotangent[3][None, :]) / (1.0 - alphas)
    return gradient_rows(params, pix_x, pix_y, dalpha * alphas, weights, weight_cot)


def composite(partials, live_mask, target_tile, valid_slot):
    slot_total = partials.shape[0]
    running = jnp.zeros(partials.shape[2:], jnp.float32)
    transmit = []
    for slot_index in range(slot_total):
        transmit.append(jnp.exp(running))
        running = running + partials[slot_index, 3]
    transmit = jnp.stack(transmit)
    shaded = transmit[:, None, :] * partials[:, :3]
    rendered = jnp.sum(shaded, axis=0) * live_mask
    residual = (rendered - target_tile) * live_mask
    behind = []
    running_sum = jnp.zeros_like(rendered)
    for slot_index in range(slot_total - 1, -1, -1):
        behind.insert(0, running_sum)
        running_sum = running_sum + shaded[slot_index]
    behind = jnp.stack(behind)
    valid_weight = valid_slot.astype(jnp.float32)
    weight_cot = transmit[:, None, :] * residual[None] * valid_weight[:, None, None]
    after_cot = jnp.sum(residual[None] * behind, axis=1) * valid_weight[:, None]
    return rendered, jnp.concatenate([weight_cot, after_cot[:, None, :]], axis=1)


def reference(gaussians, seg_count, seg_block, ray_count, camera_shift, target):
    def per_tile(grad_sum, flat_index):
        view_index = flat_index // TILES
        tile_index = flat_index % TILES
        blocks = seg_block[view_index, tile_index]
        params = gaussians[blocks]
        valid_slot = jnp.arange(SEG_MAX) < seg_count[view_index, tile_index]
        pix_x, pix_y = pixel_frame(camera_shift[view_index])
        partials = jax.vmap(partial(forward_task, pix_x=pix_x, pix_y=pix_y))(params)
        partials = jnp.where(valid_slot[:, None, None], partials, 0.0)
        live_mask = (jnp.arange(PIX) < ray_count[view_index, tile_index]).astype(jnp.float32)
        rendered, cotangent = composite(partials, live_mask, target[view_index, tile_index], valid_slot)
        grad_slots = jax.vmap(partial(backward_task, pix_x=pix_x, pix_y=pix_y))(params, cotangent)
        return grad_sum.at[blocks].add(grad_slots), rendered

    grad_sum, images = lax.scan(per_tile, jnp.zeros((BLOCKS, 9, GB), jnp.float32), jnp.arange(VIEWS * TILES))
    return images.reshape(VIEWS, TILES, 3, PIX), grad_sum
```

```python
import functools

import jax
import jax.numpy as jnp
from jax import lax
from jax.experimental import pallas as pl
from jax.experimental.pallas import tpu as pltpu
from jax.sharding import PartitionSpec as P

TILE = 48
LANES = 128
LOG2E = 1.4426950408889634
MESH = pl.DeviceIdType.MESH
F32 = jnp.float32
BF16 = jnp.bfloat16


def split(value):
    high = value.astype(BF16)
    return high, (value - high.astype(F32)).astype(BF16)


def dot(left, right):
    return jnp.dot(left, right, preferred_element_type=F32)


def dot_nt(left, right):
    return lax.dot_general(left, right, (((1,), (1,)), ((), ())), preferred_element_type=F32)


def cell_peers(cells, me):
    side = me % 2
    base = me - side
    peers = [((base + 1 - side) % cells, 0, 3 - side, 2 + side)]
    for pair in (-1, 1):
        for other in (0, 1):
            cell = (base + 2 * pair + other + cells) % cells
            peers.append((cell, pair, 2 * pair + 2 + other, side + 2 - 2 * pair))
    return peers


def pair_ids(even, odd, slots):
    count = even[0:1, 0:1]
    ids = []
    for s in range(slots + 1):
        picked = even[0:1, 1 + min(s, slots - 1) : 2 + min(s, slots - 1)]
        for k in range(slots):
            picked = jnp.where(count == s - k, odd[0:1, 1 + k : 2 + k], picked)
        ids.append(picked)
    return ids


def fetch_kernel(
    cells, slots, info_ref, gauss_ref, tgt_ref, infos, blocks, tgts, resp, got,
    info_send, info_recv, tgt_send, tgt_recv, blk_send, blk_recv,
):
    me = lax.axis_index("cell")
    side = me % 2
    per_block = gauss_ref.shape[0]
    peers = cell_peers(cells, me)
    barrier = pltpu.get_barrier_semaphore()
    for cell, _, _, _ in peers:
        pl.semaphore_signal(barrier, inc=1, device_id={"cell": cell}, device_id_type=MESH)
    pl.semaphore_wait(barrier, len(peers))
    infos[2 + side] = info_ref[...]
    sends = []
    for n, (cell, _, _, theirs) in enumerate(peers):
        copy = pltpu.make_async_remote_copy(
            info_ref, infos.at[theirs], info_send.at[n], info_recv.at[theirs],
            device_id={"cell": cell}, device_id_type=MESH,
        )
        copy.start()
        sends.append(copy)
    partner = peers[0][0]
    tgt_copy = pltpu.make_async_remote_copy(
        tgt_ref.at[1 - side], tgts.at[side], tgt_send, tgt_recv,
        device_id={"cell": partner}, device_id_type=MESH,
    )
    tgt_copy.start()
    tgts[side] = tgt_ref[side]
    for n, (cell, _, mine, _) in enumerate(peers):
        pltpu.make_async_remote_copy(
            info_ref, infos.at[mine], info_send.at[n], info_recv.at[mine],
            device_id={"cell": cell}, device_id_type=MESH,
        ).wait_recv()
    for pair in (-1, 1, 0):
        ids = pair_ids(infos[2 * pair + 2], infos[2 * pair + 3], slots)
        for s in range(slots + 1):
            local = ids[s] - me * per_block
            total = jnp.zeros(gauss_ref.shape[1:], F32)
            for b in range(per_block):
                total = jnp.where(local == b, gauss_ref[b], total)
            resp[pair + 1, s] = total
        for n, (cell, distance, _, theirs) in enumerate(peers):
            if distance == pair:
                copy = pltpu.make_async_remote_copy(
                    resp.at[pair + 1], got.at[theirs], blk_send.at[n], blk_recv.at[theirs],
                    device_id={"cell": cell}, device_id_type=MESH,
                )
                copy.start()
                sends.append(copy)
    total = resp[1]
    for n, (cell, distance, mine, _) in enumerate(peers):
        pltpu.make_async_remote_copy(
            resp.at[distance + 1], got.at[mine], blk_send.at[n], blk_recv.at[mine],
            device_id={"cell": cell}, device_id_type=MESH,
        ).wait_recv()
        total = total + got[mine]
    blocks[...] = total
    tgt_copy.wait_recv()
    tgt_copy.wait_send()
    for copy in sends:
        copy.wait_send()


def fetch(cells, slots, info, gaussians, halves):
    pack = (slots + 1,) + gaussians.shape[1:]
    vmem = pl.BlockSpec(memory_space=pltpu.VMEM)
    dma = pltpu.SemaphoreType.DMA
    return pl.pallas_call(
        functools.partial(fetch_kernel, cells, slots),
        out_shape=(
            jax.ShapeDtypeStruct((6,) + info.shape, jnp.int32),
            jax.ShapeDtypeStruct(pack, F32),
            jax.ShapeDtypeStruct(halves.shape, F32),
        ),
        in_specs=[vmem] * 3,
        out_specs=(vmem,) * 3,
        scratch_shapes=[
            pltpu.VMEM((3,) + pack, F32),
            pltpu.VMEM((6,) + pack, F32),
            dma((5,)), dma((6,)), dma, dma, dma((5,)), dma((6,)),
        ],
        compiler_params=pltpu.CompilerParams(
            collective_id=0, has_side_effects=True, vmem_limit_bytes=24 * 2**20
        ),
        name="fetch_blocks",
    )(info, gaussians, halves)


def render_kernel(
    slots, chunk, par_ref, infos, shift_ref, tgt_ref, grad_ref, img_ref, alphas, weights, w_hi, w_lo, moments, cgrads
):
    side = lax.axis_index("cell") % 2
    half = tgt_ref.shape[2]
    size = par_ref.shape[2]
    segs = slots + 1
    even, odd = infos[2], infos[3]
    count, ray_even, ray_odd = even[0:1, 0:1], even[0:1, slots + 1 : slots + 2], odd[0:1, slots + 1 : slots + 2]
    shift_x, shift_y = shift_ref[0:1, 0:1], shift_ref[0:1, 1:2]
    centre = (TILE - 1) / 2.0
    row_ids = lax.broadcasted_iota(jnp.int32, (size, size), 0)
    col_ids = lax.broadcasted_iota(jnp.int32, (size, size), 1)
    before = (row_ids < col_ids).astype(F32).astype(BF16)
    after = (row_ids > col_ids).astype(F32).astype(BF16)
    zero3 = jnp.zeros((5, size), F32)
    moments[...] = jnp.zeros_like(moments)
    cgrads[...] = jnp.zeros_like(cgrads)

    def place(ids):
        ids = ids.astype(F32)
        row = jnp.floor((ids + 0.5) * (1.0 / TILE))
        return ids - TILE * row - centre, row - centre

    def colour_rows(s):
        colours = jnp.concatenate([par_ref[s, 6:9], zero3], axis=0)
        in_even = (count > s).astype(F32)
        both = jnp.concatenate([colours * in_even, colours * (1.0 - in_even)], axis=0)
        high = both.astype(BF16).astype(F32)
        return high, both - high

    @pl.loop(0, half // chunk)
    def _(step):
        start = pl.multiple_of(step * chunk, chunk)
        first = side * half + start
        x_0, y_0 = place(first + lax.broadcasted_iota(jnp.int32, (chunk, size), 0))
        x_0 = x_0 - shift_x
        y_0 = y_0 - shift_y
        lane_ids = first + lax.broadcasted_iota(jnp.int32, (16, chunk), 1)
        carry = jnp.zeros((chunk, 1), F32)
        image = jnp.zeros((32, chunk), F32)
        for s in range(segs):
            row = lambda r: par_ref[s, r : r + 1]
            dx = x_0 - row(0)
            dy = y_0 - row(1)
            power = dx * ((-0.5 * LOG2E) * row(2) * dx + (-LOG2E) * row(3) * dy) + ((-0.5 * LOG2E) * row(4) * dy) * dy
            alpha = row(5) * jnp.exp2(power)
            ell = jnp.log(1.0 - alpha)
            high, low = split(ell)
            prefix = dot(high, before) + dot(low, before) + carry
            weight = alpha * jnp.exp(prefix)
            carry = jnp.where(count == s + 1, 0.0, prefix[:, size - 1 :] + ell[:, size - 1 :])
            high, low = split(weight)
            alphas[s] = alpha
            weights[s] = weight
            w_hi[s] = high
            w_lo[s] = low
            c_hi, c_lo = colour_rows(s)
            colours = jnp.concatenate([c_hi, c_lo], axis=0).astype(BF16)
            image = image + dot_nt(colours, high) + dot_nt(colours, low)
        in_tile = lax.broadcasted_iota(jnp.int32, (16, chunk), 0) < 8
        live = (lane_ids < jnp.where(in_tile, ray_even, ray_odd)).astype(F32)
        rendered = (image[:16] + image[16:]) * live
        cols = pl.ds(start, chunk)
        img_ref[0, :, cols] = rendered[:8]
        img_ref[1, :, cols] = rendered[8:]
        target = jnp.concatenate([tgt_ref[0, :, cols], tgt_ref[1, :, cols]], axis=0)
        residual = (rendered - target) * live
        r_hi = residual.astype(BF16).astype(F32)
        r_lo = residual - r_hi
        spread = jnp.concatenate([r_hi, r_lo, r_hi, jnp.zeros((LANES - 48, chunk), F32)], axis=0)
        spread = jnp.transpose(spread).astype(BF16)
        r_rows = jnp.concatenate([r_hi, r_lo], axis=0).astype(BF16)
        x_l, y_l = place(lane_ids[:1])
        squares = [x_l * x_l, x_l * y_l, y_l * y_l]
        sq_hi = [q.astype(BF16).astype(F32) for q in squares]
        none = jnp.zeros_like(x_l)
        features = [none + 1.0, x_l, y_l] + sq_hi + [none] * 5 + [q - h for q, h in zip(squares, sq_hi)] + [none] * 2
        features = jnp.concatenate(features, axis=0).astype(BF16)
        carry = jnp.zeros((chunk, 1), F32)
        for s in reversed(range(segs)):
            c_hi, c_lo = colour_rows(s)
            colours = jnp.concatenate([c_hi, c_hi, c_lo, jnp.zeros((LANES - 48, size), F32)], axis=0).astype(BF16)
            product = weights[s] * dot(spread, colours)
            high, low = split(product)
            tail = dot(high, after) + dot(low, after) + carry
            carry = jnp.where(count == s, 0.0, tail[:, :1] + product[:, :1])
            alpha = alphas[s]
            rest = 1.0 - alpha
            inverse = pl.reciprocal(rest, approx=True)
            inverse = inverse * (2.0 - rest * inverse)
            high, low = split(product - alpha * inverse * tail)
            moments[s] += dot(features, high) + dot(features, low)
            cgrads[s] += dot(r_rows, w_hi[s]) + dot(r_rows, w_lo[s])

    for s in range(segs):
        row = lambda r: par_ref[s, r : r + 1]
        mean_x, mean_y = row(0) + shift_x, row(1) + shift_y
        m = [moments[s, k : k + 1] for k in range(3)] + [
            moments[s, k : k + 1] + moments[s, k + 8 : k + 9] for k in range(3, 6)
        ]
        along_x = m[1] - mean_x * m[0]
        along_y = m[2] - mean_y * m[0]
        square_x = m[3] - 2.0 * mean_x * m[1] + mean_x * mean_x * m[0]
        cross_xy = m[4] - mean_x * m[2] - mean_y * m[1] + mean_x * mean_y * m[0]
        square_y = m[5] - 2.0 * mean_y * m[2] + mean_y * mean_y * m[0]
        cg = cgrads[s, :16] + cgrads[s, 16:]
        grad_ref[s, 0:1] = row(2) * along_x + row(3) * along_y
        grad_ref[s, 1:2] = row(3) * along_x + row(4) * along_y
        grad_ref[s, 2:3] = -0.5 * square_x
        grad_ref[s, 3:4] = -cross_xy
        grad_ref[s, 4:5] = -0.5 * square_y
        grad_ref[s, 5:6] = m[0] / row(5)
        grad_ref[s, 6:9] = jnp.where(count > s, cg[0:3], cg[8:11])


def render(slots, params, infos, shift, halves):
    segs, _, size = params.shape
    half = halves.shape[2]
    chunk = next(c for c in (384, 256, 128) if half % c == 0)
    vmem = pl.BlockSpec(memory_space=pltpu.VMEM)
    return pl.pallas_call(
        functools.partial(render_kernel, slots, chunk),
        out_shape=(
            jax.ShapeDtypeStruct(params.shape, F32),
            jax.ShapeDtypeStruct(halves.shape, F32),
        ),
        in_specs=[vmem] * 4,
        out_specs=(vmem,) * 2,
        scratch_shapes=[
            pltpu.VMEM((segs, chunk, size), F32),
            pltpu.VMEM((segs, chunk, size), F32),
            pltpu.VMEM((segs, chunk, size), BF16),
            pltpu.VMEM((segs, chunk, size), BF16),
            pltpu.VMEM((segs, 16, size), F32),
            pltpu.VMEM((segs, 32, size), F32),
        ],
        compiler_params=pltpu.CompilerParams(vmem_limit_bytes=40 * 2**20),
        name="render_pair",
    )(params, infos, shift, halves)


def reduce_kernel(
    cells, views, slots, grad_ref, infos, img_ref, out_ref, imgs, got, part, quarter,
    img_send, img_recv, seg_send, seg_recv, part_send, part_recv, full_send, full_recv,
):
    me = lax.axis_index("cell")
    view = lax.axis_index("view")
    side = me % 2
    per_block = out_ref.shape[0]
    share = per_block // views
    peers = cell_peers(cells, me)
    others = [(view + k) % views for k in range(1, views)]
    barrier = pltpu.get_barrier_semaphore()
    for cell, _, _, _ in peers:
        pl.semaphore_signal(barrier, inc=1, device_id={"cell": cell}, device_id_type=MESH)
    for other in others:
        pl.semaphore_signal(barrier, inc=1, device_id={"view": other}, device_id_type=MESH)
    pl.semaphore_wait(barrier, len(peers) + len(others))
    sends = []
    for n, (cell, _, _, theirs) in enumerate(peers):
        copy = pltpu.make_async_remote_copy(
            grad_ref, got.at[theirs], seg_send.at[n], seg_recv.at[theirs],
            device_id={"cell": cell}, device_id_type=MESH,
        )
        copy.start()
        sends.append(copy)
    img_copy = pltpu.make_async_remote_copy(
        img_ref.at[1 - side], imgs.at[side], img_send, img_recv,
        device_id={"cell": peers[0][0]}, device_id_type=MESH,
    )
    img_copy.start()
    imgs[side] = img_ref[side]
    for n, (cell, _, mine, _) in enumerate(peers):
        pltpu.make_async_remote_copy(
            grad_ref, got.at[mine], seg_send.at[n], seg_recv.at[mine],
            device_id={"cell": cell}, device_id_type=MESH,
        ).wait_recv()
    got[2 + side] = grad_ref[...]
    locals_, sums = [], []
    for pair in (-1, 0, 1):
        ids = pair_ids(infos[2 * pair + 2], infos[2 * pair + 3], slots)
        for s in range(slots + 1):
            locals_.append(ids[s] - me * per_block)
            sums.append((pair, s))
    for b in range(per_block):
        total = jnp.zeros(out_ref.shape[1:], F32)
        for local, (pair, s) in zip(locals_, sums):
            total = total + jnp.where(local == b, got[2 * pair + 2, s] + got[2 * pair + 3, s], 0.0)
        part[b // share, b % share] = total
    for k, other in enumerate(others):
        copy = pltpu.make_async_remote_copy(
            part.at[other], quarter.at[k], part_send.at[k], part_recv.at[k],
            device_id={"view": other}, device_id_type=MESH,
        )
        copy.start()
        sends.append(copy)
    total = part[view]
    for k in range(views - 1):
        sends[len(peers) + k].wait_recv()
        total = total + quarter[k]
    mine = pl.ds(view * share, share)
    out_ref[mine] = total
    for k, other in enumerate(others):
        copy = pltpu.make_async_remote_copy(
            out_ref.at[mine], out_ref.at[mine], full_send.at[k], full_recv.at[k],
            device_id={"view": other}, device_id_type=MESH,
        )
        copy.start()
        sends.append(copy)
    for k in range(views - 1):
        theirs = pl.ds(((view + views - 1 - k) % views) * share, share)
        pltpu.make_async_remote_copy(
            out_ref.at[theirs], out_ref.at[theirs], full_send.at[k], full_recv.at[k],
            device_id={"view": others[k]}, device_id_type=MESH,
        ).wait_recv()
    img_copy.wait_recv()
    img_copy.wait_send()
    for copy in sends:
        copy.wait_send()


def reduce_grads(cells, views, slots, shape, grads, infos, images):
    vmem = pl.BlockSpec(memory_space=pltpu.VMEM)
    dma = pltpu.SemaphoreType.DMA
    share = shape[0] // views
    return pl.pallas_call(
        functools.partial(reduce_kernel, cells, views, slots),
        out_shape=(
            jax.ShapeDtypeStruct(shape, F32),
            jax.ShapeDtypeStruct(images.shape, F32),
        ),
        in_specs=[vmem] * 3,
        out_specs=(vmem,) * 2,
        scratch_shapes=[
            pltpu.VMEM((6,) + grads.shape, F32),
            pltpu.VMEM((views, share) + shape[1:], F32),
            pltpu.VMEM((views - 1, share) + shape[1:], F32),
            dma, dma, dma((5,)), dma((6,)),
            dma((views - 1,)), dma((views - 1,)), dma((views - 1,)), dma((views - 1,)),
        ],
        compiler_params=pltpu.CompilerParams(
            collective_id=1, has_side_effects=True, vmem_limit_bytes=24 * 2**20
        ),
        name="reduce_grads",
    )(grads, infos, images)


def shards(cells, views, gaussians, seg_count, seg_block, ray_count, camera_shift, target):
    slots = seg_block.shape[2]
    pixels = target.shape[3]
    fields = jnp.concatenate([seg_count[0], seg_block[0, 0], ray_count[0]])
    info = jnp.broadcast_to(jnp.pad(fields, (0, LANES - fields.shape[0]))[None], (8, LANES))
    halves = target[0, 0].reshape(3, 2, pixels // 2).transpose(1, 0, 2)
    halves = jnp.pad(halves, ((0, 0), (0, 5), (0, 0)))
    infos, params, targets = fetch(cells, slots, info, gaussians, halves)
    grads, images = render(slots, params, infos, camera_shift, targets)
    gauss_grad, images = reduce_grads(cells, views, slots, gaussians.shape, grads, infos, images)
    image = images[:, :3].transpose(1, 0, 2).reshape(3, pixels)
    return (image[None, None], gauss_grad)


def solution(mesh):
    placed = (
        P("cell", None, None),
        P("view", "cell"),
        P("view", "cell", None),
        P("view", "cell"),
        P("view", None),
        P("view", "cell", None, None),
    )
    return jax.shard_map(
        functools.partial(shards, mesh.shape["cell"], mesh.shape["view"]),
        mesh=mesh,
        in_specs=placed,
        out_specs=(P("view", "cell", None, None), P("cell", None, None)),
        check_vma=False,
    )
```

```python
import functools

import jax
import jax.numpy as jnp
from jax import lax
from jax.experimental import pallas as pl
from jax.experimental.pallas import tpu as pltpu
from jax.sharding import PartitionSpec as P

TILE = 48
LANES = 128
LOG2E = 1.4426950408889634
MESH = pl.DeviceIdType.MESH
F32 = jnp.float32
BF16 = jnp.bfloat16


def split(value):
    high = value.astype(BF16)
    return high, (value - high.astype(F32)).astype(BF16)


def dot(left, right):
    return jnp.dot(left, right, preferred_element_type=F32)


def dot_nt(left, right):
    return lax.dot_general(left, right, (((1,), (1,)), ((), ())), preferred_element_type=F32)


def cell_peers(cells, me):
    side = me % 2
    base = me - side
    peers = [((base + 1 - side) % cells, 0, 3 - side, 2 + side)]
    for pair in (-1, 1):
        for other in (0, 1):
            cell = (base + 2 * pair + other + cells) % cells
            peers.append((cell, pair, 2 * pair + 2 + other, side + 2 - 2 * pair))
    return peers


def pair_ids(even, odd, slots):
    count = even[0:1, 0:1]
    ids = []
    for s in range(slots + 1):
        picked = even[0:1, 1 + min(s, slots - 1) : 2 + min(s, slots - 1)]
        for k in range(slots):
            picked = jnp.where(count == s - k, odd[0:1, 1 + k : 2 + k], picked)
        ids.append(picked)
    return ids


def packed_rows(blocks, rows):
    return 2 * blocks * rows


def put(ref, blocks, index, value):
    rows, size = value.shape
    for h in range(2):
        at = (h * blocks + index) * rows
        ref[at : at + rows] = value[:, h * (size // 2) : (h + 1) * (size // 2)]


def take(value, blocks, index, rows):
    parts = []
    for h in range(2):
        at = (h * blocks + index) * rows
        parts.append(value[at : at + rows])
    return jnp.concatenate(parts, axis=1)


def fetch_kernel(
    cells, slots, count_ref, block_ref, ray_ref, gauss_ref, tgt_ref, infos, blocks, tgts, info, half_out, resp, got,
    info_send, info_recv, tgt_send, tgt_recv, blk_send, blk_recv,
):
    me = lax.axis_index("cell")
    side = me % 2
    per_block, rows, _ = gauss_ref.shape
    half = tgts.shape[2]
    peers = cell_peers(cells, me)
    barrier = pltpu.get_barrier_semaphore()
    for cell, _, _, _ in peers:
        pl.semaphore_signal(barrier, inc=1, device_id={"cell": cell}, device_id_type=MESH)
    lane = lax.broadcasted_iota(jnp.int32, info.shape, 1)
    fields = jnp.where(lane == 0, count_ref[0, 0], 0)
    for s in range(slots):
        fields = jnp.where(lane == 1 + s, block_ref[0, 0, s], fields)
    fields = jnp.where(lane == 1 + slots, ray_ref[0, 0], fields)
    info[...] = fields
    infos[2 + side] = fields
    other_half = pl.multiple_of((1 - side) * half, LANES)
    own_half = pl.multiple_of(side * half, LANES)
    blank = jnp.zeros((8 - tgt_ref.shape[2], half), F32)
    half_out[...] = jnp.concatenate([tgt_ref[0, 0, :, pl.ds(other_half, half)], blank], axis=0)
    tgts[side] = jnp.concatenate([tgt_ref[0, 0, :, pl.ds(own_half, half)], blank], axis=0)
    pl.semaphore_wait(barrier, len(peers))
    sends = []
    for n, (cell, _, _, theirs) in enumerate(peers):
        copy = pltpu.make_async_remote_copy(
            info, infos.at[theirs], info_send.at[n], info_recv.at[theirs],
            device_id={"cell": cell}, device_id_type=MESH,
        )
        copy.start()
        sends.append(copy)
    tgt_copy = pltpu.make_async_remote_copy(
        half_out, tgts.at[side], tgt_send, tgt_recv,
        device_id={"cell": peers[0][0]}, device_id_type=MESH,
    )
    tgt_copy.start()
    for pair in (-1, 1, 0):
        for n, (cell, distance, mine, _) in enumerate(peers):
            if distance == pair:
                pltpu.make_async_remote_copy(
                    info, infos.at[mine], info_send.at[n], info_recv.at[mine],
                    device_id={"cell": cell}, device_id_type=MESH,
                ).wait_recv()
        ids = pair_ids(infos[2 * pair + 2], infos[2 * pair + 3], slots)
        for s in range(slots + 1):
            local = jnp.broadcast_to(ids[s] - me * per_block, gauss_ref.shape[1:])
            total = jnp.zeros(gauss_ref.shape[1:], F32)
            for b in range(per_block):
                total = jnp.where(local == b, gauss_ref[b], total)
            put(resp.at[pair + 1], slots + 1, s, total)
        for n, (cell, distance, _, theirs) in enumerate(peers):
            if distance == pair:
                copy = pltpu.make_async_remote_copy(
                    resp.at[pair + 1], got.at[theirs], blk_send.at[n], blk_recv.at[theirs],
                    device_id={"cell": cell}, device_id_type=MESH,
                )
                copy.start()
                sends.append(copy)
    total = resp[1]
    for n, (cell, distance, mine, _) in enumerate(peers):
        pltpu.make_async_remote_copy(
            resp.at[distance + 1], got.at[mine], blk_send.at[n], blk_recv.at[mine],
            device_id={"cell": cell}, device_id_type=MESH,
        ).wait_recv()
        total = total + got[mine]
    for s in range(slots + 1):
        blocks[s] = take(total, slots + 1, s, rows)
    tgt_copy.wait_recv()
    tgt_copy.wait_send()
    for copy in sends:
        copy.wait_send()


def fetch(cells, seg_count, seg_block, ray_count, gaussians, target):
    slots = seg_block.shape[2]
    _, rows, size = gaussians.shape
    half = target.shape[3] // 2
    pack = (packed_rows(slots + 1, rows), size // 2)
    vmem = pl.BlockSpec(memory_space=pltpu.VMEM)
    smem = pl.BlockSpec(memory_space=pltpu.SMEM)
    dma = pltpu.SemaphoreType.DMA
    return pl.pallas_call(
        functools.partial(fetch_kernel, cells, slots),
        out_shape=(
            jax.ShapeDtypeStruct((6, 8, LANES), jnp.int32),
            jax.ShapeDtypeStruct((slots + 1, rows, size), F32),
            jax.ShapeDtypeStruct((2, 8, half), F32),
        ),
        in_specs=[smem] * 3 + [vmem] * 2,
        out_specs=(vmem,) * 3,
        scratch_shapes=[
            pltpu.VMEM((8, LANES), jnp.int32),
            pltpu.VMEM((8, half), F32),
            pltpu.VMEM((3,) + pack, F32),
            pltpu.VMEM((6,) + pack, F32),
            dma((5,)), dma((6,)), dma, dma, dma((5,)), dma((6,)),
        ],
        compiler_params=pltpu.CompilerParams(
            collective_id=0, has_side_effects=True, vmem_limit_bytes=24 * 2**20
        ),
        name="fetch_blocks",
    )(seg_count, seg_block, ray_count, gaussians, target)


def render_kernel(
    slots, chunk, sub, par_ref, infos, shift_ref, tgt_ref, grad_ref, img_ref,
    alphas, weights, w_pair, stage, h_pair, x_pos, y_pos, moments, cgrads,
):
    side = lax.axis_index("cell") % 2
    half = tgt_ref.shape[2]
    size = par_ref.shape[2]
    segs = slots + 1
    even, odd = infos[2], infos[3]
    count, ray_even, ray_odd = even[0:1, 0:1], even[0:1, slots + 1 : slots + 2], odd[0:1, slots + 1 : slots + 2]
    shift_x, shift_y = shift_ref[0:1, 0:1], shift_ref[0:1, 1:2]
    centre = (TILE - 1) / 2.0
    row_ids = lax.broadcasted_iota(jnp.int32, (size, size), 0)
    col_ids = lax.broadcasted_iota(jnp.int32, (size, size), 1)
    before = (row_ids < col_ids).astype(F32).astype(BF16)
    after = (row_ids > col_ids).astype(F32).astype(BF16)
    before = jnp.concatenate([before, before], axis=0)
    after = jnp.concatenate([after, after], axis=0)
    blank = jnp.zeros((5, size), F32)
    moments[...] = jnp.zeros_like(moments)
    cgrads[...] = jnp.zeros_like(cgrads)
    parts = [slice(r, r + sub) for r in range(0, chunk, sub)]

    def place(ids):
        ids = ids.astype(F32)
        row = jnp.floor((ids + 0.5) * (1.0 / TILE))
        return ids - TILE * row - centre, row - centre

    def colour_rows(s):
        colours = jnp.concatenate([par_ref[s, 6:9], blank], axis=0)
        in_even = (count > s).astype(F32)
        both = jnp.concatenate([colours * in_even, colours * (1.0 - in_even)], axis=0)
        high = both.astype(BF16).astype(F32)
        return high, both - high

    @pl.loop(0, half // chunk)
    def _(step):
        start = pl.multiple_of(step * chunk, chunk)
        first = side * half + start
        for rows in parts:
            x_0, y_0 = place(first + rows.start + lax.broadcasted_iota(jnp.int32, (sub, size), 0))
            x_pos[rows] = x_0 - shift_x
            y_pos[rows] = y_0 - shift_y
        lane_ids = first + lax.broadcasted_iota(jnp.int32, (16, chunk), 1)
        carry = jnp.ones((chunk, 1), F32)
        image = jnp.zeros((32, chunk), F32)
        for s in range(segs):
            row = lambda r: par_ref[s, r : r + 1]
            mean_x, mean_y, opacity = row(0), row(1), row(5)
            k_a, k_b, k_c = (-0.5 * LOG2E) * row(2), (-LOG2E) * row(3), (-0.5 * LOG2E) * row(4)
            for rows in parts:
                dx = x_pos[rows] - mean_x
                dy = y_pos[rows] - mean_y
                alpha = opacity * jnp.exp2(dx * (k_a * dx + k_b * dy) + (k_c * dy) * dy)
                alphas[s, rows] = alpha
                high, low = split(jnp.log(1.0 - alpha))
                stage[rows, :size] = high
                stage[rows, size:] = low
            prefix = dot(stage[...], before)
            last = []
            for rows in parts:
                alpha = alphas[s, rows]
                trans = jnp.exp(prefix[rows]) * carry[rows]
                weight = alpha * trans
                weights[s, rows] = weight
                high, low = split(weight)
                w_pair[s, rows, :size] = high
                w_pair[s, rows, size:] = low
                last.append((trans - weight)[:, size - 1 :])
            carry = jnp.where(count == s + 1, 1.0, jnp.concatenate(last, axis=0))
            c_hi, c_lo = colour_rows(s)
            colours = jnp.concatenate([c_hi, c_lo], axis=0).astype(BF16)
            image = image + dot_nt(jnp.concatenate([colours, colours], axis=1), w_pair[s])
        in_tile = lax.broadcasted_iota(jnp.int32, (16, chunk), 0) < 8
        live = (lane_ids < jnp.where(in_tile, ray_even, ray_odd)).astype(F32)
        rendered = (image[:16] + image[16:]) * live
        cols = pl.ds(start, chunk)
        img_ref[0, :, cols] = rendered[:8]
        img_ref[1, :, cols] = rendered[8:]
        target = jnp.concatenate([tgt_ref[0, :, cols], tgt_ref[1, :, cols]], axis=0)
        residual = (rendered - target) * live
        r_hi = residual.astype(BF16).astype(F32)
        r_lo = residual - r_hi
        spread = jnp.concatenate([r_hi, r_lo, r_hi, jnp.zeros((LANES - 48, chunk), F32)], axis=0)
        spread = jnp.transpose(spread).astype(BF16)
        r_rows = jnp.concatenate([r_hi, r_lo], axis=0).astype(BF16)
        x_l, y_l = place(lane_ids[:1])
        squares = [x_l * x_l, x_l * y_l, y_l * y_l]
        sq_hi = [q.astype(BF16).astype(F32) for q in squares]
        none = jnp.zeros_like(x_l)
        features = [none + 1.0, x_l, y_l] + sq_hi + [none] * 5 + [q - h for q, h in zip(squares, sq_hi)] + [none] * 2
        features = jnp.concatenate(features, axis=0).astype(BF16)
        features = jnp.concatenate([features, features], axis=1)
        carry = jnp.zeros((chunk, 1), F32)
        for s in reversed(range(segs)):
            c_hi, c_lo = colour_rows(s)
            colours = jnp.concatenate([c_hi, c_hi, c_lo, jnp.zeros((LANES - 48, size), F32)], axis=0).astype(BF16)
            shaded = dot(spread, colours)
            for rows in parts:
                product = weights[s, rows] * shaded[rows]
                weights[s, rows] = product
                high, low = split(product)
                stage[rows, :size] = high
                stage[rows, size:] = low
            later = dot(stage[...], after)
            last = []
            for rows in parts:
                product = weights[s, rows]
                alpha = alphas[s, rows]
                tail = later[rows] + carry[rows]
                last.append((tail + product)[:, :1])
                rest = 1.0 - alpha
                inverse = pl.reciprocal(rest, approx=True)
                inverse = inverse * (2.0 - rest * inverse)
                high, low = split(product - alpha * inverse * tail)
                h_pair[rows] = high
                h_pair[slice(chunk + rows.start, chunk + rows.stop)] = low
            carry = jnp.where(count == s, 0.0, jnp.concatenate(last, axis=0))
            moments[s] += dot(features, h_pair[...])
            cgrads[s] += dot(r_rows, w_pair[s])

    for s in range(segs):
        row = lambda r: par_ref[s, r : r + 1]
        mean_x, mean_y = row(0) + shift_x, row(1) + shift_y
        m = [moments[s, k : k + 1] for k in range(3)] + [
            moments[s, k : k + 1] + moments[s, k + 8 : k + 9] for k in range(3, 6)
        ]
        along_x = m[1] - mean_x * m[0]
        along_y = m[2] - mean_y * m[0]
        square_x = m[3] - 2.0 * mean_x * m[1] + mean_x * mean_x * m[0]
        cross_xy = m[4] - mean_x * m[2] - mean_y * m[1] + mean_x * mean_y * m[0]
        square_y = m[5] - 2.0 * mean_y * m[2] + mean_y * mean_y * m[0]
        cg = cgrads[s, :16] + cgrads[s, 16:]
        cg = cg[:, :size] + cg[:, size:]
        grads = [
            row(2) * along_x + row(3) * along_y,
            row(3) * along_x + row(4) * along_y,
            -0.5 * square_x,
            -cross_xy,
            -0.5 * square_y,
            m[0] / row(5),
            jnp.where(count > s, cg[0:3], cg[8:11]),
        ]
        put(grad_ref, segs, s, jnp.concatenate(grads, axis=0))


def render(slots, params, infos, shift, halves):
    segs, rows, size = params.shape
    half = halves.shape[2]
    chunk = next(c for c in (384, 256, 128) if half % c == 0)
    vmem = pl.BlockSpec(memory_space=pltpu.VMEM)
    return pl.pallas_call(
        functools.partial(render_kernel, slots, chunk, 32),
        out_shape=(
            jax.ShapeDtypeStruct((packed_rows(segs, rows), size // 2), F32),
            jax.ShapeDtypeStruct(halves.shape, F32),
        ),
        in_specs=[vmem] * 4,
        out_specs=(vmem,) * 2,
        scratch_shapes=[
            pltpu.VMEM((segs, chunk, size), F32),
            pltpu.VMEM((segs, chunk, size), F32),
            pltpu.VMEM((segs, chunk, 2 * size), BF16),
            pltpu.VMEM((chunk, 2 * size), BF16),
            pltpu.VMEM((2 * chunk, size), BF16),
            pltpu.VMEM((chunk, size), F32),
            pltpu.VMEM((chunk, size), F32),
            pltpu.VMEM((segs, 16, size), F32),
            pltpu.VMEM((segs, 32, 2 * size), F32),
        ],
        compiler_params=pltpu.CompilerParams(vmem_limit_bytes=40 * 2**20),
        name="render_pair",
    )(params, infos, shift, halves)


def reduce_kernel(
    cells, views, slots, rows, grad_ref, infos, img_ref, out_ref, out_img, img_in, got, part, quarter, full,
    img_send, img_recv, seg_send, seg_recv, part_send, part_recv, full_send, full_recv,
):
    me = lax.axis_index("cell")
    view = lax.axis_index("view")
    side = me % 2
    per_block = out_ref.shape[0]
    share = per_block // views
    half = img_ref.shape[2]
    channels = out_img.shape[2]
    peers = cell_peers(cells, me)
    others = [(view + k) % views for k in range(1, views)]
    barrier = pltpu.get_barrier_semaphore()
    for cell, _, _, _ in peers:
        pl.semaphore_signal(barrier, inc=1, device_id={"cell": cell}, device_id_type=MESH)
    for other in others:
        pl.semaphore_signal(barrier, inc=1, device_id={"view": other}, device_id_type=MESH)
    pl.semaphore_wait(barrier, len(peers) + len(others))
    sends = []
    for n, (cell, _, _, theirs) in reversed(list(enumerate(peers))):
        copy = pltpu.make_async_remote_copy(
            grad_ref, got.at[theirs], seg_send.at[n], seg_recv.at[theirs],
            device_id={"cell": cell}, device_id_type=MESH,
        )
        copy.start()
        sends.append(copy)
    img_copy = pltpu.make_async_remote_copy(
        img_ref.at[1 - side], img_in, img_send, img_recv,
        device_id={"cell": peers[0][0]}, device_id_type=MESH,
    )
    img_copy.start()
    out_img[0, 0, :, pl.ds(pl.multiple_of(side * half, LANES), half)] = img_ref[side, :channels]
    ids, sums = [], []
    for pair in (0, -1, 1):
        for s, block in enumerate(pair_ids(infos[2 * pair + 2], infos[2 * pair + 3], slots)):
            ids.append(jnp.broadcast_to(block - me * per_block, out_ref.shape[1:]))
    for pair in (0, -1, 1):
        for n, (cell, distance, mine, _) in enumerate(peers):
            if distance == pair:
                pltpu.make_async_remote_copy(
                    grad_ref, got.at[mine], seg_send.at[n], seg_recv.at[mine],
                    device_id={"cell": cell}, device_id_type=MESH,
                ).wait_recv()
        if pair == 0:
            both = grad_ref[...] + got[3 - side]
        else:
            both = got[2 * pair + 2] + got[2 * pair + 3]
        sums += [take(both, slots + 1, s, rows) for s in range(slots + 1)]
    for b in range(per_block):
        total = jnp.zeros(out_ref.shape[1:], F32)
        for local, value in zip(ids, sums):
            total = total + jnp.where(local == b, value, 0.0)
        put(part.at[b // share], share, b % share, total)
    part_copies = []
    for k, other in enumerate(others):
        copy = pltpu.make_async_remote_copy(
            part.at[other], quarter.at[k], part_send.at[k], part_recv.at[k],
            device_id={"view": other}, device_id_type=MESH,
        )
        copy.start()
        part_copies.append(copy)
    total = part[view]
    for k, copy in enumerate(part_copies):
        copy.wait_recv()
        total = total + quarter[k]
    full[view] = total
    for k, other in enumerate(others):
        copy = pltpu.make_async_remote_copy(
            full.at[view], full.at[view], full_send.at[k], full_recv.at[k],
            device_id={"view": other}, device_id_type=MESH,
        )
        copy.start()
        sends.append(copy)
    img_copy.wait_recv()
    out_img[0, 0, :, pl.ds(pl.multiple_of((1 - side) * half, LANES), half)] = img_in[:channels]
    for k in range(views - 1):
        theirs = (view + views - 1 - k) % views
        pltpu.make_async_remote_copy(
            full.at[theirs], full.at[theirs], full_send.at[k], full_recv.at[k],
            device_id={"view": others[k]}, device_id_type=MESH,
        ).wait_recv()
    for b in range(per_block):
        out_ref[b] = take(full[b // share], share, b % share, rows)
    img_copy.wait_send()
    for copy in sends + part_copies:
        copy.wait_send()


def reduce_grads(cells, views, slots, shape, image_shape, grads, infos, images):
    vmem = pl.BlockSpec(memory_space=pltpu.VMEM)
    dma = pltpu.SemaphoreType.DMA
    share = shape[0] // views
    pack = (packed_rows(share, shape[1]), shape[2] // 2)
    return pl.pallas_call(
        functools.partial(reduce_kernel, cells, views, slots, shape[1]),
        out_shape=(
            jax.ShapeDtypeStruct(shape, F32),
            jax.ShapeDtypeStruct(image_shape, F32),
        ),
        in_specs=[vmem] * 3,
        out_specs=(vmem,) * 2,
        scratch_shapes=[
            pltpu.VMEM(images.shape[1:], F32),
            pltpu.VMEM((6,) + grads.shape, F32),
            pltpu.VMEM((views,) + pack, F32),
            pltpu.VMEM((views - 1,) + pack, F32),
            pltpu.VMEM((views,) + pack, F32),
            dma, dma, dma((5,)), dma((6,)),
            dma((views - 1,)), dma((views - 1,)), dma((views - 1,)), dma((views - 1,)),
        ],
        compiler_params=pltpu.CompilerParams(
            collective_id=1, has_side_effects=True, vmem_limit_bytes=24 * 2**20
        ),
        name="reduce_grads",
    )(grads, infos, images)


def shards(cells, views, gaussians, seg_count, seg_block, ray_count, camera_shift, target):
    slots = seg_block.shape[2]
    infos, params, targets = fetch(cells, seg_count, seg_block, ray_count, gaussians, target)
    grads, images = render(slots, params, infos, camera_shift, targets)
    gauss_grad, image = reduce_grads(cells, views, slots, gaussians.shape, target.shape, grads, infos, images)
    return (image, gauss_grad)


def solution(mesh):
    placed = (
        P("cell", None, None),
        P("view", "cell"),
        P("view", "cell", None),
        P("view", "cell"),
        P("view", None),
        P("view", "cell", None, None),
    )
    return jax.shard_map(
        functools.partial(shards, mesh.shape["cell"], mesh.shape["view"]),
        mesh=mesh,
        in_specs=placed,
        out_specs=(P("view", "cell", None, None), P("cell", None, None)),
        check_vma=False,
    )
```

```python
import functools

import jax
import jax.numpy as jnp
from jax import lax
from jax.experimental import pallas as pl
from jax.experimental.pallas import tpu as pltpu
from jax.sharding import PartitionSpec as P

TILE = 48
LANES = 128
LOG2E = 1.4426950408889634
MESH = pl.DeviceIdType.MESH
F32 = jnp.float32
BF16 = jnp.bfloat16


def split(value):
    high = value.astype(BF16)
    return high, (value - high.astype(F32)).astype(BF16)


def dot(left, right):
    return jnp.dot(left, right, preferred_element_type=F32)


def dot_nt(left, right):
    return lax.dot_general(left, right, (((1,), (1,)), ((), ())), preferred_element_type=F32)


def cell_peers(cells, me):
    side = me % 2
    base = me - side
    peers = [((base + 1 - side) % cells, 0, 3 - side, 2 + side)]
    for pair in (-1, 1):
        for other in (0, 1):
            cell = (base + 2 * pair + other + cells) % cells
            peers.append((cell, pair, 2 * pair + 2 + other, side + 2 - 2 * pair))
    return peers


def pair_ids(even, odd, slots):
    count = even[0:1, 0:1]
    ids = []
    for s in range(slots + 1):
        picked = even[0:1, 1 + min(s, slots - 1) : 2 + min(s, slots - 1)]
        for k in range(slots):
            picked = jnp.where(count == s - k, odd[0:1, 1 + k : 2 + k], picked)
        ids.append(picked)
    return ids


def packed_rows(blocks, rows):
    return 2 * blocks * rows


def put(ref, blocks, index, value):
    rows, size = value.shape
    for h in range(2):
        at = (h * blocks + index) * rows
        ref[at : at + rows] = value[:, h * (size // 2) : (h + 1) * (size // 2)]


def take(value, blocks, index, rows):
    parts = []
    for h in range(2):
        at = (h * blocks + index) * rows
        parts.append(value[at : at + rows])
    return jnp.concatenate(parts, axis=1)


def fetch_kernel(
    cells, slots, count_ref, block_ref, ray_ref, gauss_in, tgt_in, infos, blocks, tgts,
    gauss_ref, tgt_ref, info, half_out, resp, got, load_sem, info_send, info_recv, tgt_send, tgt_recv, blk_send, blk_recv,
):
    me = lax.axis_index("cell")
    side = me % 2
    per_block, rows, _ = gauss_ref.shape
    half = tgts.shape[2]
    peers = cell_peers(cells, me)
    tgt_load = pltpu.make_async_copy(tgt_in, tgt_ref, load_sem.at[0])
    tgt_load.start()
    gauss_load = pltpu.make_async_copy(gauss_in, gauss_ref, load_sem.at[1])
    gauss_load.start()
    barrier = pltpu.get_barrier_semaphore()
    for cell, _, _, _ in peers:
        pl.semaphore_signal(barrier, inc=1, device_id={"cell": cell}, device_id_type=MESH)
    lane = lax.broadcasted_iota(jnp.int32, info.shape, 1)
    fields = jnp.where(lane == 0, count_ref[0, 0], 0)
    for s in range(slots):
        fields = jnp.where(lane == 1 + s, block_ref[0, 0, s], fields)
    fields = jnp.where(lane == 1 + slots, ray_ref[0, 0], fields)
    info[...] = fields
    infos[2 + side] = fields
    tgt_load.wait()
    other_half = pl.multiple_of((1 - side) * half, LANES)
    own_half = pl.multiple_of(side * half, LANES)
    blank = jnp.zeros((8 - tgt_ref.shape[2], half), F32)
    half_out[...] = jnp.concatenate([tgt_ref[0, 0, :, pl.ds(other_half, half)], blank], axis=0)
    tgts[side] = jnp.concatenate([tgt_ref[0, 0, :, pl.ds(own_half, half)], blank], axis=0)
    pl.semaphore_wait(barrier, len(peers))
    sends = []
    for n, (cell, _, _, theirs) in enumerate(peers):
        copy = pltpu.make_async_remote_copy(
            info, infos.at[theirs], info_send.at[n], info_recv.at[theirs],
            device_id={"cell": cell}, device_id_type=MESH,
        )
        copy.start()
        sends.append(copy)
    tgt_copy = pltpu.make_async_remote_copy(
        half_out, tgts.at[side], tgt_send, tgt_recv,
        device_id={"cell": peers[0][0]}, device_id_type=MESH,
    )
    tgt_copy.start()
    gauss_load.wait()
    for pair in (-1, 1, 0):
        for n, (cell, distance, mine, _) in enumerate(peers):
            if distance == pair:
                pltpu.make_async_remote_copy(
                    info, infos.at[mine], info_send.at[n], info_recv.at[mine],
                    device_id={"cell": cell}, device_id_type=MESH,
                ).wait_recv()
        ids = pair_ids(infos[2 * pair + 2], infos[2 * pair + 3], slots)
        for s in range(slots + 1):
            local = jnp.broadcast_to(ids[s] - me * per_block, gauss_ref.shape[1:])
            total = jnp.zeros(gauss_ref.shape[1:], F32)
            for b in range(per_block):
                total = jnp.where(local == b, gauss_ref[b], total)
            put(resp.at[pair + 1], slots + 1, s, total)
        for n, (cell, distance, _, theirs) in enumerate(peers):
            if distance == pair:
                copy = pltpu.make_async_remote_copy(
                    resp.at[pair + 1], got.at[theirs], blk_send.at[n], blk_recv.at[theirs],
                    device_id={"cell": cell}, device_id_type=MESH,
                )
                copy.start()
                sends.append(copy)
    total = resp[1]
    for n, (cell, distance, mine, _) in enumerate(peers):
        pltpu.make_async_remote_copy(
            resp.at[distance + 1], got.at[mine], blk_send.at[n], blk_recv.at[mine],
            device_id={"cell": cell}, device_id_type=MESH,
        ).wait_recv()
        total = total + got[mine]
    for s in range(slots + 1):
        blocks[s] = take(total, slots + 1, s, rows)
    tgt_copy.wait_recv()
    tgt_copy.wait_send()
    for copy in sends:
        copy.wait_send()


def fetch(cells, seg_count, seg_block, ray_count, gaussians, target):
    slots = seg_block.shape[2]
    _, rows, size = gaussians.shape
    half = target.shape[3] // 2
    pack = (packed_rows(slots + 1, rows), size // 2)
    vmem = pl.BlockSpec(memory_space=pltpu.VMEM)
    smem = pl.BlockSpec(memory_space=pltpu.SMEM)
    dma = pltpu.SemaphoreType.DMA
    return pl.pallas_call(
        functools.partial(fetch_kernel, cells, slots),
        out_shape=(
            jax.ShapeDtypeStruct((6, 8, LANES), jnp.int32),
            jax.ShapeDtypeStruct((slots + 1, rows, size), F32),
            jax.ShapeDtypeStruct((2, 8, half), F32),
        ),
        in_specs=[smem] * 3 + [pl.BlockSpec(memory_space=pl.ANY)] * 2,
        out_specs=(vmem,) * 3,
        scratch_shapes=[
            pltpu.VMEM(gaussians.shape, F32),
            pltpu.VMEM(target.shape, F32),
            pltpu.VMEM((8, LANES), jnp.int32),
            pltpu.VMEM((8, half), F32),
            pltpu.VMEM((3,) + pack, F32),
            pltpu.VMEM((6,) + pack, F32),
            dma((2,)), dma((5,)), dma((6,)), dma, dma, dma((5,)), dma((6,)),
        ],
        compiler_params=pltpu.CompilerParams(
            collective_id=0, has_side_effects=True, vmem_limit_bytes=24 * 2**20
        ),
        name="fetch_blocks",
    )(seg_count, seg_block, ray_count, gaussians, target)


def render_kernel(
    slots, chunk, sub, par_ref, infos, shift_ref, tgt_ref, grad_ref, img_ref,
    alphas, weights, w_pair, stage, h_pair, moments, cgrads,
):
    side = lax.axis_index("cell") % 2
    half = tgt_ref.shape[2]
    size = par_ref.shape[2]
    segs = slots + 1
    even, odd = infos[2], infos[3]
    count, ray_even, ray_odd = even[0:1, 0:1], even[0:1, slots + 1 : slots + 2], odd[0:1, slots + 1 : slots + 2]
    shift_x, shift_y = shift_ref[0:1, 0:1], shift_ref[0:1, 1:2]
    centre = (TILE - 1) / 2.0
    row_ids = lax.broadcasted_iota(jnp.int32, (size, size), 0)
    col_ids = lax.broadcasted_iota(jnp.int32, (size, size), 1)
    before = (row_ids < col_ids).astype(F32).astype(BF16)
    after = (row_ids > col_ids).astype(F32).astype(BF16)
    before = jnp.concatenate([before, before], axis=0)
    after = jnp.concatenate([after, after], axis=0)
    blank = jnp.zeros((5, size), F32)
    moments[...] = jnp.zeros_like(moments)
    cgrads[...] = jnp.zeros_like(cgrads)
    parts = [slice(r, r + sub) for r in range(0, chunk, sub)]

    def place(ids):
        ids = ids.astype(F32)
        row = jnp.floor((ids + 0.5) * (1.0 / TILE))
        return ids - TILE * row - centre, row - centre

    def at(s, rows):
        return slice(s * chunk + rows.start, s * chunk + rows.stop)

    whole = slice(0, chunk)
    image_rows, shade_rows = [], []
    for s in range(segs):
        colours = jnp.concatenate([par_ref[s, 6:9], blank], axis=0)
        in_even = (count > s).astype(F32)
        both = jnp.concatenate([colours * in_even, colours * (1.0 - in_even)], axis=0)
        c_hi = both.astype(BF16).astype(F32)
        c_lo = both - c_hi
        rows = jnp.concatenate([c_hi, c_lo], axis=0).astype(BF16)
        image_rows.append(jnp.concatenate([rows, rows], axis=1))
        shade_rows.append(
            jnp.concatenate([c_hi, c_hi, c_lo, jnp.zeros((LANES - 48, size), F32)], axis=0).astype(BF16)
        )
    shade_rows = jnp.concatenate(shade_rows, axis=1)

    def steps(c):
        cols = slice(c * chunk, (c + 1) * chunk)
        first = side * half + c * chunk
        for rows in parts:
            x_0, y_0 = place(first + rows.start + lax.broadcasted_iota(jnp.int32, (sub, size), 0))
            x_0, y_0 = x_0 - shift_x, y_0 - shift_y
            for s in range(segs):
                row = lambda r: par_ref[s, r : r + 1]
                dx = x_0 - row(0)
                dy = y_0 - row(1)
                power = dx * ((-0.5 * LOG2E) * row(2) * dx + (-LOG2E) * row(3) * dy)
                alpha = row(5) * jnp.exp2(power + ((-0.5 * LOG2E) * row(4) * dy) * dy)
                alphas[c, at(s, rows)] = alpha
                high, low = split(jnp.log(1.0 - alpha))
                stage[c, at(s, rows), :size] = high
                stage[c, at(s, rows), size:] = low
        yield
        prefix = dot(stage[c], before)
        yield
        for rows in parts:
            carry = jnp.ones((sub, 1), F32)
            for s in range(segs):
                alpha = alphas[c, at(s, rows)]
                trans = jnp.exp(prefix[at(s, rows)]) * carry
                weight = alpha * trans
                weights[c, at(s, rows)] = weight
                high, low = split(weight)
                w_pair[c, at(s, rows), :size] = high
                w_pair[c, at(s, rows), size:] = low
                carry = jnp.where(count == s + 1, 1.0, (trans - weight)[:, size - 1 :])
        yield
        image = jnp.zeros((32, chunk), F32)
        for s in range(segs):
            image = image + dot_nt(image_rows[s], w_pair[c, at(s, whole)])
        yield
        in_tile = lax.broadcasted_iota(jnp.int32, (16, chunk), 0) < 8
        lane_ids = first + lax.broadcasted_iota(jnp.int32, (16, chunk), 1)
        live = (lane_ids < jnp.where(in_tile, ray_even, ray_odd)).astype(F32)
        rendered = (image[:16] + image[16:]) * live
        img_ref[0, :, cols] = rendered[:8]
        img_ref[1, :, cols] = rendered[8:]
        target = jnp.concatenate([tgt_ref[0, :, cols], tgt_ref[1, :, cols]], axis=0)
        residual = (rendered - target) * live
        r_hi = residual.astype(BF16).astype(F32)
        r_lo = residual - r_hi
        spread = jnp.concatenate([r_hi, r_lo, r_hi, jnp.zeros((LANES - 48, chunk), F32)], axis=0)
        spread = jnp.transpose(spread).astype(BF16)
        r_rows = jnp.concatenate([r_hi, r_lo], axis=0).astype(BF16)
        x_l, y_l = place(lane_ids[:1])
        squares = [x_l * x_l, x_l * y_l, y_l * y_l]
        sq_hi = [q.astype(BF16).astype(F32) for q in squares]
        none = jnp.zeros_like(x_l)
        features = [none + 1.0, x_l, y_l] + sq_hi + [none] * 5 + [q - h for q, h in zip(squares, sq_hi)] + [none] * 2
        features = jnp.concatenate(features, axis=0).astype(BF16)
        features = jnp.concatenate([features, features], axis=1)
        shaded = dot(spread, shade_rows)
        yield
        for rows in parts:
            for s in range(segs):
                product = weights[c, at(s, rows)] * shaded[rows, s * size : (s + 1) * size]
                weights[c, at(s, rows)] = product
                high, low = split(product)
                stage[c, at(s, rows), :size] = high
                stage[c, at(s, rows), size:] = low
        yield
        later = dot(stage[c], after)
        for s in range(segs):
            cgrads[s] += dot(r_rows, w_pair[c, at(s, whole)])
        yield
        for rows in parts:
            carry = jnp.zeros((sub, 1), F32)
            for s in reversed(range(segs)):
                product = weights[c, at(s, rows)]
                alpha = alphas[c, at(s, rows)]
                tail = later[at(s, rows)] + carry
                carry = jnp.where(count == s, 0.0, (tail + product)[:, :1])
                rest = 1.0 - alpha
                inverse = pl.reciprocal(rest, approx=True)
                inverse = inverse * (2.0 - rest * inverse)
                high, low = split(product - alpha * inverse * tail)
                h_pair[c, s, rows] = high
                h_pair[c, s, slice(chunk + rows.start, chunk + rows.stop)] = low
        yield
        for s in range(segs):
            moments[s] += dot(features, h_pair[c, s])
        yield

    chunks = [steps(c) for c in range(half // chunk)]
    for tick in range(9 + len(chunks) - 1):
        for c, stages in enumerate(chunks):
            if 0 <= tick - c < 9:
                next(stages)

    for s in range(segs):
        row = lambda r: par_ref[s, r : r + 1]
        mean_x, mean_y = row(0) + shift_x, row(1) + shift_y
        m = [moments[s, k : k + 1] for k in range(3)] + [
            moments[s, k : k + 1] + moments[s, k + 8 : k + 9] for k in range(3, 6)
        ]
        along_x = m[1] - mean_x * m[0]
        along_y = m[2] - mean_y * m[0]
        square_x = m[3] - 2.0 * mean_x * m[1] + mean_x * mean_x * m[0]
        cross_xy = m[4] - mean_x * m[2] - mean_y * m[1] + mean_x * mean_y * m[0]
        square_y = m[5] - 2.0 * mean_y * m[2] + mean_y * mean_y * m[0]
        cg = cgrads[s, :16] + cgrads[s, 16:]
        cg = cg[:, :size] + cg[:, size:]
        grads = [
            row(2) * along_x + row(3) * along_y,
            row(3) * along_x + row(4) * along_y,
            -0.5 * square_x,
            -cross_xy,
            -0.5 * square_y,
            m[0] / row(5),
            jnp.where(count > s, cg[0:3], cg[8:11]),
        ]
        put(grad_ref, segs, s, jnp.concatenate(grads, axis=0))


def render(slots, params, infos, shift, halves):
    segs, rows, size = params.shape
    half = halves.shape[2]
    chunk = next(c for c in (384, 256, 128) if half % c == 0)
    steps = half // chunk
    vmem = pl.BlockSpec(memory_space=pltpu.VMEM)
    return pl.pallas_call(
        functools.partial(render_kernel, slots, chunk, 32),
        out_shape=(
            jax.ShapeDtypeStruct((packed_rows(segs, rows), size // 2), F32),
            jax.ShapeDtypeStruct(halves.shape, F32),
        ),
        in_specs=[vmem] * 4,
        out_specs=(vmem,) * 2,
        scratch_shapes=[
            pltpu.VMEM((steps, segs * chunk, size), F32),
            pltpu.VMEM((steps, segs * chunk, size), F32),
            pltpu.VMEM((steps, segs * chunk, 2 * size), BF16),
            pltpu.VMEM((steps, segs * chunk, 2 * size), BF16),
            pltpu.VMEM((steps, segs, 2 * chunk, size), BF16),
            pltpu.VMEM((segs, 16, size), F32),
            pltpu.VMEM((segs, 32, 2 * size), F32),
        ],
        compiler_params=pltpu.CompilerParams(vmem_limit_bytes=54 * 2**20),
        name="render_pair",
    )(params, infos, shift, halves)


def reduce_kernel(
    cells, views, slots, rows, grad_ref, infos, img_ref, out_ref, out_img, img_in, got, part, quarter, full,
    img_send, img_recv, seg_send, seg_recv, part_send, part_recv, full_send, full_recv,
):
    me = lax.axis_index("cell")
    view = lax.axis_index("view")
    side = me % 2
    per_block = out_ref.shape[0]
    share = per_block // views
    half = img_ref.shape[2]
    channels = out_img.shape[2]
    peers = cell_peers(cells, me)
    others = [(view + k) % views for k in range(1, views)]
    barrier = pltpu.get_barrier_semaphore()
    for cell, _, _, _ in peers:
        pl.semaphore_signal(barrier, inc=1, device_id={"cell": cell}, device_id_type=MESH)
    for other in others:
        pl.semaphore_signal(barrier, inc=1, device_id={"view": other}, device_id_type=MESH)
    pl.semaphore_wait(barrier, len(peers) + len(others))
    sends = []
    for n, (cell, _, _, theirs) in reversed(list(enumerate(peers))):
        copy = pltpu.make_async_remote_copy(
            grad_ref, got.at[theirs], seg_send.at[n], seg_recv.at[theirs],
            device_id={"cell": cell}, device_id_type=MESH,
        )
        copy.start()
        sends.append(copy)
    img_copy = pltpu.make_async_remote_copy(
        img_ref.at[1 - side], img_in, img_send, img_recv,
        device_id={"cell": peers[0][0]}, device_id_type=MESH,
    )
    img_copy.start()
    out_img[0, 0, :, pl.ds(pl.multiple_of(side * half, LANES), half)] = img_ref[side, :channels]
    ids, sums = [], []
    for pair in (0, -1, 1):
        for s, block in enumerate(pair_ids(infos[2 * pair + 2], infos[2 * pair + 3], slots)):
            ids.append(jnp.broadcast_to(block - me * per_block, out_ref.shape[1:]))
    for pair in (0, -1, 1):
        for n, (cell, distance, mine, _) in enumerate(peers):
            if distance == pair:
                pltpu.make_async_remote_copy(
                    grad_ref, got.at[mine], seg_send.at[n], seg_recv.at[mine],
                    device_id={"cell": cell}, device_id_type=MESH,
                ).wait_recv()
        if pair == 0:
            both = grad_ref[...] + got[3 - side]
        else:
            both = got[2 * pair + 2] + got[2 * pair + 3]
        sums += [take(both, slots + 1, s, rows) for s in range(slots + 1)]
    for b in range(per_block):
        total = jnp.zeros(out_ref.shape[1:], F32)
        for local, value in zip(ids, sums):
            total = total + jnp.where(local == b, value, 0.0)
        put(part.at[b // share], share, b % share, total)
    part_copies = []
    for k, other in enumerate(others):
        copy = pltpu.make_async_remote_copy(
            part.at[other], quarter.at[k], part_send.at[k], part_recv.at[k],
            device_id={"view": other}, device_id_type=MESH,
        )
        copy.start()
        part_copies.append(copy)
    total = part[view]
    for k, copy in enumerate(part_copies):
        copy.wait_recv()
        total = total + quarter[k]
    full[view] = total
    for k, other in enumerate(others):
        copy = pltpu.make_async_remote_copy(
            full.at[view], full.at[view], full_send.at[k], full_recv.at[k],
            device_id={"view": other}, device_id_type=MESH,
        )
        copy.start()
        sends.append(copy)
    img_copy.wait_recv()
    out_img[0, 0, :, pl.ds(pl.multiple_of((1 - side) * half, LANES), half)] = img_in[:channels]
    for k in range(views - 1):
        theirs = (view + views - 1 - k) % views
        pltpu.make_async_remote_copy(
            full.at[theirs], full.at[theirs], full_send.at[k], full_recv.at[k],
            device_id={"view": others[k]}, device_id_type=MESH,
        ).wait_recv()
    for b in range(per_block):
        out_ref[b] = take(full[b // share], share, b % share, rows)
    img_copy.wait_send()
    for copy in sends + part_copies:
        copy.wait_send()


def reduce_grads(cells, views, slots, shape, image_shape, grads, infos, images):
    vmem = pl.BlockSpec(memory_space=pltpu.VMEM)
    dma = pltpu.SemaphoreType.DMA
    share = shape[0] // views
    pack = (packed_rows(share, shape[1]), shape[2] // 2)
    return pl.pallas_call(
        functools.partial(reduce_kernel, cells, views, slots, shape[1]),
        out_shape=(
            jax.ShapeDtypeStruct(shape, F32),
            jax.ShapeDtypeStruct(image_shape, F32),
        ),
        in_specs=[vmem] * 3,
        out_specs=(vmem,) * 2,
        scratch_shapes=[
            pltpu.VMEM(images.shape[1:], F32),
            pltpu.VMEM((6,) + grads.shape, F32),
            pltpu.VMEM((views,) + pack, F32),
            pltpu.VMEM((views - 1,) + pack, F32),
            pltpu.VMEM((views,) + pack, F32),
            dma, dma, dma((5,)), dma((6,)),
            dma((views - 1,)), dma((views - 1,)), dma((views - 1,)), dma((views - 1,)),
        ],
        compiler_params=pltpu.CompilerParams(
            collective_id=1, has_side_effects=True, vmem_limit_bytes=24 * 2**20
        ),
        name="reduce_grads",
    )(grads, infos, images)


def shards(cells, views, gaussians, seg_count, seg_block, ray_count, camera_shift, target):
    slots = seg_block.shape[2]
    infos, params, targets = fetch(cells, seg_count, seg_block, ray_count, gaussians, target)
    grads, images = render(slots, params, infos, camera_shift, targets)
    gauss_grad, image = reduce_grads(cells, views, slots, gaussians.shape, target.shape, grads, infos, images)
    return (image, gauss_grad)


def solution(mesh):
    placed = (
        P("cell", None, None),
        P("view", "cell"),
        P("view", "cell", None),
        P("view", "cell"),
        P("view", None),
        P("view", "cell", None, None),
    )
    return jax.shard_map(
        functools.partial(shards, mesh.shape["cell"], mesh.shape["view"]),
        mesh=mesh,
        in_specs=placed,
        out_specs=(P("view", "cell", None, None), P("cell", None, None)),
        check_vma=False,
    )
```

```python
import functools

import jax
import jax.numpy as jnp
from jax import lax
from jax.experimental import pallas as pl
from jax.experimental.pallas import tpu as pltpu
from jax.sharding import PartitionSpec as P

TILE = 48
LANES = 128
LOG2E = 1.4426950408889634
MESH = pl.DeviceIdType.MESH
F32 = jnp.float32
BF16 = jnp.bfloat16


def split(value):
    high = value.astype(BF16)
    return high, (value - high.astype(F32)).astype(BF16)


def dot(left, right):
    return jnp.dot(left, right, preferred_element_type=F32)


def dot_nt(left, right):
    return lax.dot_general(left, right, (((1,), (1,)), ((), ())), preferred_element_type=F32)


def cell_peers(cells, me):
    side = me % 2
    base = me - side
    peers = [((base + 1 - side) % cells, 0, 3 - side, 2 + side)]
    for pair in (-1, 1):
        for other in (0, 1):
            cell = (base + 2 * pair + other + cells) % cells
            peers.append((cell, pair, 2 * pair + 2 + other, side + 2 - 2 * pair))
    return peers


def pair_ids(even, odd, slots):
    count = even[0:1, 0:1]
    ids = []
    for s in range(slots + 1):
        picked = even[0:1, 1 + min(s, slots - 1) : 2 + min(s, slots - 1)]
        for k in range(slots):
            picked = jnp.where(count == s - k, odd[0:1, 1 + k : 2 + k], picked)
        ids.append(picked)
    return ids


def over(value, divisor):
    return jnp.floor((value + 0.5) * (1.0 / divisor))


def iota(shape, axis):
    return lax.broadcasted_iota(jnp.int32, shape, axis).astype(F32)


def round_up(value, unit):
    return -(-value // unit) * unit


def step_kernel(
    cells, views, slots, rows, chunk, sub,
    count_ref, block_ref, ray_ref, shift_ref, gauss_in, tgt_in, out_ref, out_img,
    gauss_ref, gauss_parts, tgt_ref, tgts, info, infos, half_out, resp, got, par_ref, grad_ref, got_grad,
    img_out, img_in, part, quarter, full, alphas, weights, w_pair, stage, h_pair, moments, cgrads,
    load_sem, info_send, info_recv, tgt_send, tgt_recv, blk_send, blk_recv,
    img_send, img_recv, seg_send, seg_recv, part_send, part_recv, full_send, full_recv,
):
    me = lax.axis_index("cell")
    view = lax.axis_index("view")
    side = me % 2
    segs = slots + 1
    dense_rows, size = gauss_ref.shape
    per_block = dense_rows // rows
    pack = par_ref.shape[0]
    half = tgts.shape[2]
    channels = tgt_ref.shape[0]
    peers = cell_peers(cells, me)
    others = [(view + k) % views for k in range(1, views)]

    def to_cell(src, dst, send, recv, cell):
        return pltpu.make_async_remote_copy(
            src, dst, send, recv, device_id={"cell": cell}, device_id_type=MESH
        )

    def to_view(src, dst, send, recv, other):
        return pltpu.make_async_remote_copy(
            src, dst, send, recv, device_id={"view": other}, device_id_type=MESH
        )

    gauss_load = pltpu.make_async_copy(gauss_in, gauss_ref, load_sem.at[0])
    gauss_load.start()
    tgt_load = pltpu.make_async_copy(tgt_in, tgt_ref, load_sem.at[1])
    tgt_load.start()
    barrier = pltpu.get_barrier_semaphore()
    for cell, _, _, _ in peers:
        pl.semaphore_signal(barrier, inc=1, device_id={"cell": cell}, device_id_type=MESH)
    for other in others:
        pl.semaphore_signal(barrier, inc=1, device_id={"view": other}, device_id_type=MESH)
    lane = lax.broadcasted_iota(jnp.int32, info.shape, 1)
    fields = jnp.where(lane == 0, count_ref[0, 0], 0)
    for s in range(slots):
        fields = jnp.where(lane == 1 + s, block_ref[0, 0, s], fields)
    fields = jnp.where(lane == 1 + slots, ray_ref[0, 0], fields)
    info[...] = fields
    infos[2 + side] = fields
    gauss_load.wait()
    gauss = gauss_ref[...]
    high = gauss.astype(BF16)
    rest = gauss - high.astype(F32)
    middle = rest.astype(BF16)
    gauss_parts[:dense_rows] = high
    gauss_parts[dense_rows : 2 * dense_rows] = middle
    gauss_parts[2 * dense_rows : 3 * dense_rows] = (rest - middle.astype(F32)).astype(BF16)
    spare = gauss_parts.shape[0] - 3 * dense_rows
    if spare:
        gauss_parts[3 * dense_rows :] = jnp.zeros((spare, size), BF16)
    tgt_load.wait()
    blank = jnp.zeros((8 - channels, half), F32)

    def tile_half(which):
        cols = pl.ds(pl.multiple_of(which * half, LANES), half)
        return jnp.concatenate([tgt_ref[r, :, cols] for r in range(channels)] + [blank], axis=0)

    half_out[...] = tile_half(1 - side)
    tgts[side] = tile_half(side)
    moments[...] = jnp.zeros_like(moments)
    cgrads[...] = jnp.zeros_like(cgrads)
    pl.semaphore_wait(barrier, len(peers) + len(others))

    sends = []
    for n, (cell, _, _, theirs) in reversed(list(enumerate(peers))):
        sends.append(to_cell(info, infos.at[theirs], info_send.at[n], info_recv.at[theirs], cell))
        sends[-1].start()
    tgt_copy = to_cell(half_out, tgts.at[side], tgt_send, tgt_recv, peers[0][0])
    tgt_copy.start()

    row_id = iota((pack, gauss_parts.shape[0]), 0)
    row_param = over(row_id, segs)
    row_slot = row_id - segs * row_param
    lane_id = iota((pack, gauss_parts.shape[0]), 1)
    lane_part = over(lane_id, dense_rows)
    lane_id = lane_id - dense_rows * lane_part
    lane_param = over(lane_id, per_block)
    same = (row_param == lane_param) & (lane_part < 3.0)
    lane_block = lane_id - per_block * lane_param
    local = {}
    for pair in (-1, 1, 0):
        for n, (cell, distance, mine, _) in enumerate(peers):
            if distance == pair:
                to_cell(info, infos.at[mine], info_send.at[n], info_recv.at[mine], cell).wait_recv()
        ids = pair_ids(infos[2 * pair + 2], infos[2 * pair + 3], slots)
        local[pair] = [(block - me * per_block).astype(F32) for block in ids]
        wanted = jnp.full(row_id.shape, -1.0, F32)
        for s in range(segs):
            wanted = jnp.where(row_slot == float(s), local[pair][s], wanted)
        chosen = jnp.where(same & (lane_block == wanted), 1.0, 0.0).astype(BF16)
        resp[pair + 1] = dot(chosen, gauss_parts[...])
        for n, (cell, distance, _, theirs) in enumerate(peers):
            if distance == pair:
                sends.append(to_cell(resp.at[pair + 1], got.at[theirs], blk_send.at[n], blk_recv.at[theirs], cell))
                sends[-1].start()

    even, odd = infos[2], infos[3]
    count, ray_even, ray_odd = even[0:1, 0:1], even[0:1, slots + 1 : slots + 2], odd[0:1, slots + 1 : slots + 2]
    shift_x, shift_y = shift_ref[0:1, 0:1], shift_ref[0:1, 1:2]
    centre = (TILE - 1) / 2.0
    row_ids = lax.broadcasted_iota(jnp.int32, (size, size), 0)
    col_ids = lax.broadcasted_iota(jnp.int32, (size, size), 1)
    before = (row_ids < col_ids).astype(F32).astype(BF16)
    after = (row_ids > col_ids).astype(F32).astype(BF16)
    before = jnp.concatenate([before, before], axis=0)
    after = jnp.concatenate([after, after], axis=0)
    parts = [slice(r, r + sub) for r in range(0, chunk, sub)]
    whole = slice(0, chunk)
    dense_row = iota((dense_rows, round_up(3 * pack, LANES)), 0)
    dense_param = over(dense_row, per_block)
    dense_block = dense_row - per_block * dense_param
    pack_lane = iota(dense_row.shape, 1)
    pack_pair = over(pack_lane, pack)
    pack_lane = pack_lane - pack * pack_pair
    pack_param = over(pack_lane, segs)
    pack_slot = pack_lane - segs * pack_param
    wanted = jnp.full(dense_row.shape, -1.0, F32)
    for pair in (-1, 0, 1):
        for s in range(segs):
            here = (pack_pair == float(pair + 1)) & (pack_slot == float(s))
            wanted = jnp.where(here, local[pair][s], wanted)
    placing = jnp.where((dense_param == pack_param) & (dense_block == wanted), 1.0, 0.0).astype(BF16)

    total = resp[1]
    for n, (cell, distance, mine, _) in enumerate(peers):
        to_cell(resp.at[distance + 1], got.at[mine], blk_send.at[n], blk_recv.at[mine], cell).wait_recv()
        total = total + got[mine]
    par_ref[...] = total
    tgt_copy.wait_recv()

    def param(s, r):
        return par_ref[r * segs + s : r * segs + s + 1]

    def place(ids):
        ids = ids.astype(F32)
        row = over(ids, TILE)
        return ids - TILE * row - centre, row - centre

    def at(s, rows):
        return slice(s * chunk + rows.start, s * chunk + rows.stop)

    image_rows, shade_rows = [], []
    for s in range(segs):
        colours = jnp.concatenate([param(s, 6 + r) for r in range(3)] + [jnp.zeros((5, size), F32)], axis=0)
        in_even = (count > s).astype(F32)
        both = jnp.concatenate([colours * in_even, colours * (1.0 - in_even)], axis=0)
        c_hi = both.astype(BF16).astype(F32)
        c_lo = both - c_hi
        pieces = jnp.concatenate([c_hi, c_lo], axis=0).astype(BF16)
        image_rows.append(jnp.concatenate([pieces, pieces], axis=1))
        shade_rows.append(
            jnp.concatenate([c_hi, c_hi, c_lo, jnp.zeros((LANES - 48, size), F32)], axis=0).astype(BF16)
        )
    shade_rows = jnp.concatenate(shade_rows, axis=1)

    def steps(c):
        cols = slice(c * chunk, (c + 1) * chunk)
        first = side * half + c * chunk
        for rows in parts:
            x_0, y_0 = place(first + rows.start + lax.broadcasted_iota(jnp.int32, (sub, size), 0))
            x_0, y_0 = x_0 - shift_x, y_0 - shift_y
            for s in range(segs):
                row = functools.partial(param, s)
                dx = x_0 - row(0)
                dy = y_0 - row(1)
                power = dx * ((-0.5 * LOG2E) * row(2) * dx + (-LOG2E) * row(3) * dy)
                alpha = row(5) * jnp.exp2(power + ((-0.5 * LOG2E) * row(4) * dy) * dy)
                alphas[c, at(s, rows)] = alpha
                high, low = split(jnp.log(1.0 - alpha))
                stage[c, at(s, rows), :size] = high
                stage[c, at(s, rows), size:] = low
        yield
        prefix = dot(stage[c], before)
        yield
        for rows in parts:
            carry = jnp.ones((sub, 1), F32)
            for s in range(segs):
                alpha = alphas[c, at(s, rows)]
                trans = jnp.exp(prefix[at(s, rows)]) * carry
                weight = alpha * trans
                weights[c, at(s, rows)] = weight
                high, low = split(weight)
                w_pair[c, at(s, rows), :size] = high
                w_pair[c, at(s, rows), size:] = low
                carry = jnp.where(count == s + 1, 1.0, (trans - weight)[:, size - 1 :])
        yield
        image = jnp.zeros((32, chunk), F32)
        for s in range(segs):
            image = image + dot_nt(image_rows[s], w_pair[c, at(s, whole)])
        yield
        in_tile = lax.broadcasted_iota(jnp.int32, (16, chunk), 0) < 8
        lane_ids = first + lax.broadcasted_iota(jnp.int32, (16, chunk), 1)
        live = (lane_ids < jnp.where(in_tile, ray_even, ray_odd)).astype(F32)
        rendered = (image[:16] + image[16:]) * live
        own = jnp.where(side == 0, rendered[:8], rendered[8:])
        img_out[:, cols] = jnp.where(side == 0, rendered[8:], rendered[:8])
        for r in range(channels):
            out_img[r, :, pl.ds(pl.multiple_of(first, LANES), chunk)] = own[r : r + 1]
        target = jnp.concatenate([tgts[0, :, cols], tgts[1, :, cols]], axis=0)
        residual = (rendered - target) * live
        r_hi = residual.astype(BF16).astype(F32)
        r_lo = residual - r_hi
        spread = jnp.concatenate([r_hi, r_lo, r_hi, jnp.zeros((LANES - 48, chunk), F32)], axis=0)
        spread = jnp.transpose(spread).astype(BF16)
        r_rows = jnp.concatenate([r_hi, r_lo], axis=0).astype(BF16)
        x_l, y_l = place(lane_ids[:1])
        squares = [x_l * x_l, x_l * y_l, y_l * y_l]
        sq_hi = [q.astype(BF16).astype(F32) for q in squares]
        none = jnp.zeros_like(x_l)
        features = [none + 1.0, x_l, y_l] + sq_hi + [none] * 5 + [q - h for q, h in zip(squares, sq_hi)] + [none] * 2
        features = jnp.concatenate(features, axis=0).astype(BF16)
        features = jnp.concatenate([features, features], axis=1)
        shaded = dot(spread, shade_rows)
        yield
        for rows in parts:
            for s in range(segs):
                product = weights[c, at(s, rows)] * shaded[rows, s * size : (s + 1) * size]
                weights[c, at(s, rows)] = product
                high, low = split(product)
                stage[c, at(s, rows), :size] = high
                stage[c, at(s, rows), size:] = low
        yield
        later = dot(stage[c], after)
        for s in range(segs):
            cgrads[s] += dot(r_rows, w_pair[c, at(s, whole)])
        yield
        for rows in parts:
            carry = jnp.zeros((sub, 1), F32)
            for s in reversed(range(segs)):
                product = weights[c, at(s, rows)]
                alpha = alphas[c, at(s, rows)]
                tail = later[at(s, rows)] + carry
                carry = jnp.where(count == s, 0.0, (tail + product)[:, :1])
                rest = 1.0 - alpha
                inverse = pl.reciprocal(rest, approx=True)
                inverse = inverse * (2.0 - rest * inverse)
                high, low = split(product - alpha * inverse * tail)
                h_pair[c, s, rows] = high
                h_pair[c, s, slice(chunk + rows.start, chunk + rows.stop)] = low
        yield
        for s in range(segs):
            moments[s] += dot(features, h_pair[c, s])
        yield

    chunks = [steps(c) for c in range(half // chunk)]
    for tick in range(9 + len(chunks) - 1):
        for c, stages in enumerate(chunks):
            if 0 <= tick - c < 9:
                next(stages)

    img_copy = to_cell(img_out, img_in, img_send, img_recv, peers[0][0])
    img_copy.start()
    grad_ref[...] = jnp.zeros_like(grad_ref)
    for s in range(segs):
        row = functools.partial(param, s)
        mean_x, mean_y = row(0) + shift_x, row(1) + shift_y
        m = [moments[s, k : k + 1] for k in range(3)] + [
            moments[s, k : k + 1] + moments[s, k + 8 : k + 9] for k in range(3, 6)
        ]
        along_x = m[1] - mean_x * m[0]
        along_y = m[2] - mean_y * m[0]
        square_x = m[3] - 2.0 * mean_x * m[1] + mean_x * mean_x * m[0]
        cross_xy = m[4] - mean_x * m[2] - mean_y * m[1] + mean_x * mean_y * m[0]
        square_y = m[5] - 2.0 * mean_y * m[2] + mean_y * mean_y * m[0]
        cg = cgrads[s, :16] + cgrads[s, 16:]
        cg = cg[:, :size] + cg[:, size:]
        grads = [
            row(2) * along_x + row(3) * along_y,
            row(3) * along_x + row(4) * along_y,
            -0.5 * square_x,
            -cross_xy,
            -0.5 * square_y,
            m[0] / row(5),
            jnp.where(count > s, cg[0:3], cg[8:11]),
        ]
        for r, value in enumerate(grads[:6] + [grads[6][k : k + 1] for k in range(3)]):
            grad_ref[r * segs + s : r * segs + s + 1] = value

    for n, (cell, _, _, theirs) in reversed(list(enumerate(peers))):
        sends.append(to_cell(grad_ref, got_grad.at[theirs], seg_send.at[n], seg_recv.at[theirs], cell))
        sends[-1].start()
    sums = {}
    for pair in (0, -1, 1):
        for n, (cell, distance, mine, _) in enumerate(peers):
            if distance == pair:
                to_cell(grad_ref, got_grad.at[mine], seg_send.at[n], seg_recv.at[mine], cell).wait_recv()
        if pair == 0:
            sums[pair] = grad_ref[...] + got_grad[3 - side]
        else:
            sums[pair] = got_grad[2 * pair + 2] + got_grad[2 * pair + 3]
    spare = placing.shape[1] - 3 * pack
    stacked = [sums[-1], sums[0], sums[1]] + ([jnp.zeros((spare, size), F32)] if spare else [])
    high, low = split(jnp.concatenate(stacked, axis=0))
    dense = dot(placing, high) + dot(placing, low)
    part[:dense_rows] = dense[:, : size // 2]
    part[dense_rows:] = dense[:, size // 2 :]

    share = part.shape[0] // views

    def share_of(which):
        return pl.ds(pl.multiple_of(which * share, 8), share)

    part_copies = []
    for k, other in enumerate(others):
        part_copies.append(to_view(part.at[share_of(other)], quarter.at[k], part_send.at[k], part_recv.at[k], other))
        part_copies[-1].start()
    total = part[share_of(view)]
    for k, copy in enumerate(part_copies):
        copy.wait_recv()
        total = total + quarter[k]
    full[share_of(view)] = total
    for k, other in enumerate(others):
        mine = full.at[share_of(view)]
        sends.append(to_view(mine, mine, full_send.at[k], full_recv.at[k], other))
        sends[-1].start()
    img_copy.wait_recv()
    for r in range(channels):
        out_img[r, :, pl.ds(pl.multiple_of((1 - side) * half, LANES), half)] = img_in[r : r + 1]
    for k in range(views - 1):
        theirs = full.at[share_of((view + views - 1 - k) % views)]
        to_view(theirs, theirs, full_send.at[k], full_recv.at[k], others[k]).wait_recv()
    out_ref[:, : size // 2] = full[:dense_rows]
    out_ref[:, size // 2 :] = full[dense_rows:]
    for copy in sends + part_copies + [tgt_copy, img_copy]:
        copy.wait_send()


def step(cells, views, seg_count, seg_block, ray_count, shift, gaussians, target, rows):
    slots = seg_block.shape[2]
    segs = slots + 1
    dense_rows, size = gaussians.shape
    half = target.shape[2] // 2
    chunk = next(c for c in (384, 256, 128) if half % c == 0)
    count = half // chunk
    pack = (round_up(rows * segs, 8), size)
    share = 2 * dense_rows // views
    vmem = pl.BlockSpec(memory_space=pltpu.VMEM)
    smem = pl.BlockSpec(memory_space=pltpu.SMEM)
    hbm = pl.BlockSpec(memory_space=pl.ANY)
    dma = pltpu.SemaphoreType.DMA
    return pl.pallas_call(
        functools.partial(step_kernel, cells, views, slots, rows, chunk, chunk),
        out_shape=(
            jax.ShapeDtypeStruct(gaussians.shape, F32),
            jax.ShapeDtypeStruct(target.shape, F32),
        ),
        in_specs=[smem] * 3 + [vmem] + [hbm] * 2,
        out_specs=(vmem,) * 2,
        scratch_shapes=[
            pltpu.VMEM(gaussians.shape, F32),
            pltpu.VMEM((round_up(3 * dense_rows, LANES), size), BF16),
            pltpu.VMEM(target.shape, F32),
            pltpu.VMEM((2, 8, half), F32),
            pltpu.VMEM((8, LANES), jnp.int32),
            pltpu.VMEM((6, 8, LANES), jnp.int32),
            pltpu.VMEM((8, half), F32),
            pltpu.VMEM((3,) + pack, F32),
            pltpu.VMEM((6,) + pack, F32),
            pltpu.VMEM(pack, F32),
            pltpu.VMEM(pack, F32),
            pltpu.VMEM((6,) + pack, F32),
            pltpu.VMEM((8, half), F32),
            pltpu.VMEM((8, half), F32),
            pltpu.VMEM((2 * dense_rows, size // 2), F32),
            pltpu.VMEM((views - 1, share, size // 2), F32),
            pltpu.VMEM((2 * dense_rows, size // 2), F32),
            pltpu.VMEM((count, segs * chunk, size), F32),
            pltpu.VMEM((count, segs * chunk, size), F32),
            pltpu.VMEM((count, segs * chunk, 2 * size), BF16),
            pltpu.VMEM((count, segs * chunk, 2 * size), BF16),
            pltpu.VMEM((count, segs, 2 * chunk, size), BF16),
            pltpu.VMEM((segs, 16, size), F32),
            pltpu.VMEM((segs, 32, 2 * size), F32),
            dma((2,)), dma((5,)), dma((6,)), dma, dma, dma((5,)), dma((6,)),
            dma, dma, dma((5,)), dma((6,)),
            dma((views - 1,)), dma((views - 1,)), dma((views - 1,)), dma((views - 1,)),
        ],
        compiler_params=pltpu.CompilerParams(
            collective_id=0, has_side_effects=True, vmem_limit_bytes=54 * 2**20
        ),
        name="splat_step",
    )(seg_count, seg_block, ray_count, shift, gaussians, target)


def shards(cells, views, gaussians, seg_count, seg_block, ray_count, camera_shift, target):
    blocks, rows, size = gaussians.shape
    by_row = gaussians.transpose(1, 0, 2).reshape(rows * blocks, size)
    planes = target.reshape(target.shape[2], 1, target.shape[3])
    grads, image = step(cells, views, seg_count, seg_block, ray_count, camera_shift, by_row, planes, rows)
    return (image.reshape(target.shape), grads.reshape(rows, blocks, size).transpose(1, 0, 2))


def solution(mesh):
    placed = (
        P("cell", None, None),
        P("view", "cell"),
        P("view", "cell", None),
        P("view", "cell"),
        P("view", None),
        P("view", "cell", None, None),
    )
    return jax.shard_map(
        functools.partial(shards, mesh.shape["cell"], mesh.shape["view"]),
        mesh=mesh,
        in_specs=placed,
        out_specs=(P("view", "cell", None, None), P("cell", None, None)),
        check_vma=False,
    )
```

```python
import functools

import jax
import jax.numpy as jnp
from jax import lax
from jax.experimental import pallas as pl
from jax.experimental.pallas import tpu as pltpu
from jax.sharding import PartitionSpec as P

TILE = 48
LANES = 128
LOG2E = 1.4426950408889634
MESH = pl.DeviceIdType.MESH
F32 = jnp.float32
BF16 = jnp.bfloat16


def split(value):
    high = value.astype(BF16)
    return high, (value - high.astype(F32)).astype(BF16)


def dot(left, right):
    return jnp.dot(left, right, preferred_element_type=F32)


def dot_nt(left, right):
    return lax.dot_general(left, right, (((1,), (1,)), ((), ())), preferred_element_type=F32)


def cell_peers(cells, me):
    side = me % 2
    base = me - side
    peers = [((base + 1 - side) % cells, 0, 3 - side, 2 + side)]
    for pair in (-1, 1):
        for other in (0, 1):
            cell = (base + 2 * pair + other + cells) % cells
            peers.append((cell, pair, 2 * pair + 2 + other, side + 2 - 2 * pair))
    return peers


def pair_ids(even, odd, slots):
    count = even[0:1, 0:1]
    ids = []
    for s in range(slots + 1):
        picked = even[0:1, 1 + min(s, slots - 1) : 2 + min(s, slots - 1)]
        for k in range(slots):
            picked = jnp.where(count == s - k, odd[0:1, 1 + k : 2 + k], picked)
        ids.append(picked)
    return ids


def over(value, divisor):
    return jnp.floor((value + 0.5) * (1.0 / divisor))


def iota(shape, axis):
    return lax.broadcasted_iota(jnp.int32, shape, axis).astype(F32)


def round_up(value, unit):
    return -(-value // unit) * unit


def step_kernel(
    cells, views, slots, rows, chunk, sub,
    count_ref, block_ref, ray_ref, shift_ref, gauss_in, tgt_in, full, out_img,
    gauss_ref, gauss_parts, tgt_ref, tgts, info, infos, half_out, resp, got, par_ref, grad_ref, got_grad,
    img_out, img_in, part, quarter, alphas, weights, w_pair, stage, h_pair, moments, cgrads, flat_x, delta_x, cross_y, flat_y,
    load_sem, info_send, info_recv, tgt_send, tgt_recv, blk_send, blk_recv,
    img_send, img_recv, seg_send, seg_recv, part_send, part_recv, full_send, full_recv,
):
    me = lax.axis_index("cell")
    view = lax.axis_index("view")
    side = me % 2
    segs = slots + 1
    dense_rows, size = gauss_ref.shape
    per_block = dense_rows // rows
    pack = par_ref.shape[0]
    half = tgts.shape[2]
    channels = tgt_ref.shape[0]
    peers = cell_peers(cells, me)
    others = [(view + k) % views for k in range(1, views)]

    def to_cell(src, dst, send, recv, cell):
        return pltpu.make_async_remote_copy(
            src, dst, send, recv, device_id={"cell": cell}, device_id_type=MESH
        )

    def to_view(src, dst, send, recv, other):
        return pltpu.make_async_remote_copy(
            src, dst, send, recv, device_id={"view": other}, device_id_type=MESH
        )

    gauss_load = pltpu.make_async_copy(gauss_in, gauss_ref, load_sem.at[0])
    gauss_load.start()
    tgt_load = pltpu.make_async_copy(tgt_in, tgt_ref, load_sem.at[1])
    tgt_load.start()
    barrier = pltpu.get_barrier_semaphore()
    for cell, _, _, _ in peers:
        pl.semaphore_signal(barrier, inc=1, device_id={"cell": cell}, device_id_type=MESH)
    for other in others:
        pl.semaphore_signal(barrier, inc=1, device_id={"view": other}, device_id_type=MESH)
    lane = lax.broadcasted_iota(jnp.int32, info.shape, 1)
    fields = jnp.where(lane == 0, count_ref[0, 0], 0)
    for s in range(slots):
        fields = jnp.where(lane == 1 + s, block_ref[0, 0, s], fields)
    fields = jnp.where(lane == 1 + slots, ray_ref[0, 0], fields)
    info[...] = fields
    infos[2 + side] = fields
    gauss_load.wait()
    gauss = gauss_ref[...]
    high = gauss.astype(BF16)
    rest = gauss - high.astype(F32)
    middle = rest.astype(BF16)
    gauss_parts[:dense_rows] = high
    gauss_parts[dense_rows : 2 * dense_rows] = middle
    gauss_parts[2 * dense_rows : 3 * dense_rows] = (rest - middle.astype(F32)).astype(BF16)
    spare = gauss_parts.shape[0] - 3 * dense_rows
    if spare:
        gauss_parts[3 * dense_rows :] = jnp.zeros((spare, size), BF16)
    tgt_load.wait()
    blank = jnp.zeros((8 - channels, half), F32)

    def tile_half(which):
        cols = pl.ds(pl.multiple_of(which * half, LANES), half)
        return jnp.concatenate([tgt_ref[r, :, cols] for r in range(channels)] + [blank], axis=0)

    half_out[...] = tile_half(1 - side)
    tgts[side] = tile_half(side)
    moments[...] = jnp.zeros_like(moments)
    cgrads[...] = jnp.zeros_like(cgrads)
    pl.semaphore_wait(barrier, len(peers) + len(others))

    sends = []
    for n, (cell, _, _, theirs) in reversed(list(enumerate(peers))):
        sends.append(to_cell(info, infos.at[theirs], info_send.at[n], info_recv.at[theirs], cell))
        sends[-1].start()
    tgt_copy = to_cell(half_out, tgts.at[side], tgt_send, tgt_recv, peers[0][0])
    tgt_copy.start()

    row_id = iota((pack, gauss_parts.shape[0]), 0)
    row_param = over(row_id, segs)
    row_slot = row_id - segs * row_param
    lane_id = iota((pack, gauss_parts.shape[0]), 1)
    lane_part = over(lane_id, dense_rows)
    lane_id = lane_id - dense_rows * lane_part
    lane_param = over(lane_id, per_block)
    same = (row_param == lane_param) & (lane_part < 3.0)
    lane_block = lane_id - per_block * lane_param
    local = {}
    for pair in (-1, 1, 0):
        for n, (cell, distance, mine, _) in enumerate(peers):
            if distance == pair:
                to_cell(info, infos.at[mine], info_send.at[n], info_recv.at[mine], cell).wait_recv()
        ids = pair_ids(infos[2 * pair + 2], infos[2 * pair + 3], slots)
        local[pair] = [(block - me * per_block).astype(F32) for block in ids]
        wanted = jnp.full(row_id.shape, -1.0, F32)
        for s in range(segs):
            wanted = jnp.where(row_slot == float(s), local[pair][s], wanted)
        chosen = jnp.where(same & (lane_block == wanted), 1.0, 0.0).astype(BF16)
        resp[pair + 1] = dot(chosen, gauss_parts[...])
        for n, (cell, distance, _, theirs) in enumerate(peers):
            if distance == pair:
                sends.append(to_cell(resp.at[pair + 1], got.at[theirs], blk_send.at[n], blk_recv.at[theirs], cell))
                sends[-1].start()

    even, odd = infos[2], infos[3]
    count, ray_even, ray_odd = even[0:1, 0:1], even[0:1, slots + 1 : slots + 2], odd[0:1, slots + 1 : slots + 2]
    shift_x, shift_y = shift_ref[0:1, 0:1], shift_ref[0:1, 1:2]
    centre = (TILE - 1) / 2.0
    row_ids = lax.broadcasted_iota(jnp.int32, (size, size), 0)
    col_ids = lax.broadcasted_iota(jnp.int32, (size, size), 1)
    before = (row_ids < col_ids).astype(F32).astype(BF16)
    after = (row_ids > col_ids).astype(F32).astype(BF16)
    before = jnp.concatenate([before, before], axis=0)
    after = jnp.concatenate([after, after], axis=0)
    parts = [slice(r, r + sub) for r in range(0, chunk, sub)]
    whole = slice(0, chunk)
    dense_row = iota((dense_rows, round_up(3 * pack, LANES)), 0)
    dense_param = over(dense_row, per_block)
    dense_block = dense_row - per_block * dense_param
    pack_lane = iota(dense_row.shape, 1)
    pack_pair = over(pack_lane, pack)
    pack_lane = pack_lane - pack * pack_pair
    pack_param = over(pack_lane, segs)
    pack_slot = pack_lane - segs * pack_param
    wanted = jnp.full(dense_row.shape, -1.0, F32)
    for pair in (-1, 0, 1):
        for s in range(segs):
            here = (pack_pair == float(pair + 1)) & (pack_slot == float(s))
            wanted = jnp.where(here, local[pair][s], wanted)
    placing = jnp.where((dense_param == pack_param) & (dense_block == wanted), 1.0, 0.0).astype(BF16)

    total = resp[1]
    for n, (cell, distance, mine, _) in enumerate(peers):
        to_cell(resp.at[distance + 1], got.at[mine], blk_send.at[n], blk_recv.at[mine], cell).wait_recv()
        total = total + got[mine]
    par_ref[...] = total
    tgt_copy.wait_recv()

    def param(s, r):
        return par_ref[r * segs + s : r * segs + s + 1]

    def place(ids):
        ids = ids.astype(F32)
        row = over(ids, TILE)
        return ids - TILE * row - centre, row - centre

    def at(s, rows):
        return slice(s * chunk + rows.start, s * chunk + rows.stop)

    image_rows, shade_rows = [], []
    for s in range(segs):
        colours = jnp.concatenate([param(s, 6 + r) for r in range(3)] + [jnp.zeros((5, size), F32)], axis=0)
        in_even = (count > s).astype(F32)
        both = jnp.concatenate([colours * in_even, colours * (1.0 - in_even)], axis=0)
        c_hi = both.astype(BF16).astype(F32)
        c_lo = both - c_hi
        pieces = jnp.concatenate([c_hi, c_lo], axis=0).astype(BF16)
        image_rows.append(jnp.concatenate([pieces, pieces], axis=1))
        shade_rows.append(
            jnp.concatenate([c_hi, c_hi, c_lo, jnp.zeros((LANES - 48, size), F32)], axis=0).astype(BF16)
        )
    shade_rows = jnp.concatenate(shade_rows, axis=1)
    x_0 = iota((TILE, size), 0) - centre - shift_x
    y_0 = iota(flat_y.shape[1:], 0) + (side * (half // TILE)).astype(F32) - centre - shift_y
    for s in range(segs):
        dx = x_0 - param(s, 0)
        dy = y_0 - param(s, 1)
        delta_x[s] = dx
        flat_x[s] = ((-0.5 * LOG2E) * param(s, 2)) * dx * dx + LOG2E * jnp.log(param(s, 5))
        cross_y[s] = (-LOG2E) * param(s, 3) * dy
        flat_y[s] = ((-0.5 * LOG2E) * param(s, 4)) * dy * dy

    def steps(c):
        cols = slice(c * chunk, (c + 1) * chunk)
        first = side * half + c * chunk
        for s in range(segs):
            for k in range(chunk // TILE):
                rows = slice(k * TILE, (k + 1) * TILE)
                r = c * (chunk // TILE) + k
                power = flat_x[s] + delta_x[s] * cross_y[s, r : r + 1] + flat_y[s, r : r + 1]
                alpha = jnp.exp2(power)
                alphas[c, at(s, rows)] = alpha
                high, low = split(jnp.log(1.0 - alpha))
                stage[c, at(s, rows), :size] = high
                stage[c, at(s, rows), size:] = low
        yield
        prefix = dot(stage[c], before)
        yield
        for rows in parts:
            carry = jnp.ones((sub, 1), F32)
            for s in range(segs):
                alpha = alphas[c, at(s, rows)]
                trans = jnp.exp(prefix[at(s, rows)]) * carry
                weight = alpha * trans
                weights[c, at(s, rows)] = weight
                high, low = split(weight)
                w_pair[c, at(s, rows), :size] = high
                w_pair[c, at(s, rows), size:] = low
                carry = jnp.where(count == s + 1, 1.0, (trans - weight)[:, size - 1 :])
        yield
        image = jnp.zeros((32, chunk), F32)
        for s in range(segs):
            image = image + dot_nt(image_rows[s], w_pair[c, at(s, whole)])
        yield
        in_tile = lax.broadcasted_iota(jnp.int32, (16, chunk), 0) < 8
        lane_ids = first + lax.broadcasted_iota(jnp.int32, (16, chunk), 1)
        live = (lane_ids < jnp.where(in_tile, ray_even, ray_odd)).astype(F32)
        rendered = (image[:16] + image[16:]) * live
        own = jnp.where(side == 0, rendered[:8], rendered[8:])
        img_out[:, cols] = jnp.where(side == 0, rendered[8:], rendered[:8])
        for r in range(channels):
            out_img[r, :, pl.ds(pl.multiple_of(first, LANES), chunk)] = own[r : r + 1]
        target = jnp.concatenate([tgts[0, :, cols], tgts[1, :, cols]], axis=0)
        residual = (rendered - target) * live
        r_hi = residual.astype(BF16).astype(F32)
        r_lo = residual - r_hi
        spread = jnp.concatenate([r_hi, r_lo, r_hi, jnp.zeros((LANES - 48, chunk), F32)], axis=0)
        spread = jnp.transpose(spread).astype(BF16)
        r_rows = jnp.concatenate([r_hi, r_lo], axis=0).astype(BF16)
        x_l, y_l = place(lane_ids[:1])
        squares = [x_l * x_l, x_l * y_l, y_l * y_l]
        sq_hi = [q.astype(BF16).astype(F32) for q in squares]
        none = jnp.zeros_like(x_l)
        features = [none + 1.0, x_l, y_l] + sq_hi + [none] * 5 + [q - h for q, h in zip(squares, sq_hi)] + [none] * 2
        features = jnp.concatenate(features, axis=0).astype(BF16)
        features = jnp.concatenate([features, features], axis=1)
        shaded = dot(spread, shade_rows)
        yield
        for rows in parts:
            for s in range(segs):
                product = weights[c, at(s, rows)] * shaded[rows, s * size : (s + 1) * size]
                weights[c, at(s, rows)] = product
                high, low = split(product)
                stage[c, at(s, rows), :size] = high
                stage[c, at(s, rows), size:] = low
        yield
        later = dot(stage[c], after)
        for s in range(segs):
            cgrads[s] += dot(r_rows, w_pair[c, at(s, whole)])
        yield
        for rows in parts:
            carry = jnp.zeros((sub, 1), F32)
            for s in reversed(range(segs)):
                product = weights[c, at(s, rows)]
                alpha = alphas[c, at(s, rows)]
                tail = later[at(s, rows)] + carry
                carry = jnp.where(count == s, 0.0, (tail + product)[:, :1])
                rest = 1.0 - alpha
                inverse = pl.reciprocal(rest, approx=True)
                inverse = inverse * (2.0 - rest * inverse)
                high, low = split(product - alpha * inverse * tail)
                h_pair[c, s, rows] = high
                h_pair[c, s, slice(chunk + rows.start, chunk + rows.stop)] = low
        yield
        for s in range(segs):
            moments[s] += dot(features, h_pair[c, s])
        yield

    chunks = [steps(c) for c in range(half // chunk)]
    for tick in range(9 + len(chunks) - 1):
        for c, stages in enumerate(chunks):
            if 0 <= tick - c < 9:
                next(stages)

    img_copy = to_cell(img_out, img_in, img_send, img_recv, peers[0][0])
    img_copy.start()
    grad_ref[...] = jnp.zeros_like(grad_ref)
    for s in range(segs):
        row = functools.partial(param, s)
        mean_x, mean_y = row(0) + shift_x, row(1) + shift_y
        m = [moments[s, k : k + 1] for k in range(3)] + [
            moments[s, k : k + 1] + moments[s, k + 8 : k + 9] for k in range(3, 6)
        ]
        along_x = m[1] - mean_x * m[0]
        along_y = m[2] - mean_y * m[0]
        square_x = m[3] - 2.0 * mean_x * m[1] + mean_x * mean_x * m[0]
        cross_xy = m[4] - mean_x * m[2] - mean_y * m[1] + mean_x * mean_y * m[0]
        square_y = m[5] - 2.0 * mean_y * m[2] + mean_y * mean_y * m[0]
        cg = cgrads[s, :16] + cgrads[s, 16:]
        cg = cg[:, :size] + cg[:, size:]
        grads = [
            row(2) * along_x + row(3) * along_y,
            row(3) * along_x + row(4) * along_y,
            -0.5 * square_x,
            -cross_xy,
            -0.5 * square_y,
            m[0] / row(5),
            jnp.where(count > s, cg[0:3], cg[8:11]),
        ]
        for r, value in enumerate(grads[:6] + [grads[6][k : k + 1] for k in range(3)]):
            grad_ref[r * segs + s : r * segs + s + 1] = value

    for n, (cell, _, _, theirs) in reversed(list(enumerate(peers))):
        sends.append(to_cell(grad_ref, got_grad.at[theirs], seg_send.at[n], seg_recv.at[theirs], cell))
        sends[-1].start()
    sums = {}
    for pair in (0, -1, 1):
        for n, (cell, distance, mine, _) in enumerate(peers):
            if distance == pair:
                to_cell(grad_ref, got_grad.at[mine], seg_send.at[n], seg_recv.at[mine], cell).wait_recv()
        if pair == 0:
            sums[pair] = grad_ref[...] + got_grad[3 - side]
        else:
            sums[pair] = got_grad[2 * pair + 2] + got_grad[2 * pair + 3]
    spare = placing.shape[1] - 3 * pack
    stacked = [sums[-1], sums[0], sums[1]] + ([jnp.zeros((spare, size), F32)] if spare else [])
    high, low = split(jnp.concatenate(stacked, axis=0))
    dense = dot(placing, high) + dot(placing, low)
    part[:dense_rows] = dense[:, : size // 2]
    part[dense_rows:] = dense[:, size // 2 :]

    share = part.shape[0] // views

    def share_of(which):
        return pl.ds(pl.multiple_of(which * share, 8), share)

    part_copies = []
    for k, other in enumerate(others):
        part_copies.append(to_view(part.at[share_of(other)], quarter.at[k], part_send.at[k], part_recv.at[k], other))
        part_copies[-1].start()
    total = part[share_of(view)]
    for k, copy in enumerate(part_copies):
        copy.wait_recv()
        total = total + quarter[k]
    full[share_of(view)] = total
    for k, other in enumerate(others):
        mine = full.at[share_of(view)]
        sends.append(to_view(mine, mine, full_send.at[k], full_recv.at[k], other))
        sends[-1].start()
    img_copy.wait_recv()
    for r in range(channels):
        out_img[r, :, pl.ds(pl.multiple_of((1 - side) * half, LANES), half)] = img_in[r : r + 1]
    for k in range(views - 1):
        theirs = full.at[share_of((view + views - 1 - k) % views)]
        to_view(theirs, theirs, full_send.at[k], full_recv.at[k], others[k]).wait_recv()
    for copy in sends + part_copies + [tgt_copy, img_copy]:
        copy.wait_send()


def step(cells, views, seg_count, seg_block, ray_count, shift, gaussians, target, rows):
    slots = seg_block.shape[2]
    segs = slots + 1
    dense_rows, size = gaussians.shape
    half = target.shape[2] // 2
    chunk = next(c for c in (384, half) if half % c == 0)
    count = half // chunk
    pack = (round_up(rows * segs, 8), size)
    share = 2 * dense_rows // views
    vmem = pl.BlockSpec(memory_space=pltpu.VMEM)
    smem = pl.BlockSpec(memory_space=pltpu.SMEM)
    hbm = pl.BlockSpec(memory_space=pl.ANY)
    dma = pltpu.SemaphoreType.DMA
    return pl.pallas_call(
        functools.partial(step_kernel, cells, views, slots, rows, chunk, chunk),
        out_shape=(
            jax.ShapeDtypeStruct((2 * dense_rows, size // 2), F32),
            jax.ShapeDtypeStruct(target.shape, F32),
        ),
        in_specs=[smem] * 3 + [vmem] + [hbm] * 2,
        out_specs=(vmem,) * 2,
        scratch_shapes=[
            pltpu.VMEM(gaussians.shape, F32),
            pltpu.VMEM((round_up(3 * dense_rows, LANES), size), BF16),
            pltpu.VMEM(target.shape, F32),
            pltpu.VMEM((2, 8, half), F32),
            pltpu.VMEM((8, LANES), jnp.int32),
            pltpu.VMEM((6, 8, LANES), jnp.int32),
            pltpu.VMEM((8, half), F32),
            pltpu.VMEM((3,) + pack, F32),
            pltpu.VMEM((6,) + pack, F32),
            pltpu.VMEM(pack, F32),
            pltpu.VMEM(pack, F32),
            pltpu.VMEM((6,) + pack, F32),
            pltpu.VMEM((8, half), F32),
            pltpu.VMEM((8, half), F32),
            pltpu.VMEM((2 * dense_rows, size // 2), F32),
            pltpu.VMEM((views - 1, share, size // 2), F32),
            pltpu.VMEM((count, segs * chunk, size), F32),
            pltpu.VMEM((count, segs * chunk, size), F32),
            pltpu.VMEM((count, segs * chunk, 2 * size), BF16),
            pltpu.VMEM((count, segs * chunk, 2 * size), BF16),
            pltpu.VMEM((count, segs, 2 * chunk, size), BF16),
            pltpu.VMEM((segs, 16, size), F32),
            pltpu.VMEM((segs, 32, 2 * size), F32),
            pltpu.VMEM((segs, TILE, size), F32),
            pltpu.VMEM((segs, TILE, size), F32),
            pltpu.VMEM((segs, half // TILE, size), F32),
            pltpu.VMEM((segs, half // TILE, size), F32),
            dma((2,)), dma((5,)), dma((6,)), dma, dma, dma((5,)), dma((6,)),
            dma, dma, dma((5,)), dma((6,)),
            dma((views - 1,)), dma((views - 1,)), dma((views - 1,)), dma((views - 1,)),
        ],
        compiler_params=pltpu.CompilerParams(
            collective_id=0, has_side_effects=True, vmem_limit_bytes=54 * 2**20
        ),
        name="splat_step",
    )(seg_count, seg_block, ray_count, shift, gaussians, target)


def finish_kernel(full, image, out_ref, out_img, sems):
    rows, size = out_ref.shape
    copies = [pltpu.make_async_copy(image, out_img, sems.at[0])]
    for h in range(2):
        lanes = out_ref.at[:, h * (size // 2) : (h + 1) * (size // 2)]
        copies.append(pltpu.make_async_copy(full.at[h * rows : (h + 1) * rows], lanes, sems.at[1 + h]))
    for copy in copies:
        copy.start()
    for copy in copies:
        copy.wait()


def finish(full, image):
    anywhere = pl.BlockSpec(memory_space=pl.ANY)
    return pl.pallas_call(
        finish_kernel,
        out_shape=(
            jax.ShapeDtypeStruct((full.shape[0] // 2, 2 * full.shape[1]), F32),
            jax.ShapeDtypeStruct(image.shape, F32),
        ),
        in_specs=[anywhere] * 2,
        out_specs=(anywhere,) * 2,
        scratch_shapes=[pltpu.SemaphoreType.DMA((3,))],
        compiler_params=pltpu.CompilerParams(vmem_limit_bytes=60 * 2**20),
        name="place_results",
    )(full, image)


def shards(cells, views, gaussians, seg_count, seg_block, ray_count, camera_shift, target):
    blocks, rows, size = gaussians.shape
    by_row = gaussians.transpose(1, 0, 2).reshape(rows * blocks, size)
    planes = target.reshape(target.shape[2], 1, target.shape[3])
    grads, image = step(cells, views, seg_count, seg_block, ray_count, camera_shift, by_row, planes, rows)
    grads, image = finish(grads, image)
    return (image.reshape(target.shape), grads.reshape(rows, blocks, size).transpose(1, 0, 2))


def solution(mesh):
    placed = (
        P("cell", None, None),
        P("view", "cell"),
        P("view", "cell", None),
        P("view", "cell"),
        P("view", None),
        P("view", "cell", None, None),
    )
    return jax.shard_map(
        functools.partial(shards, mesh.shape["cell"], mesh.shape["view"]),
        mesh=mesh,
        in_specs=placed,
        out_specs=(P("view", "cell", None, None), P("cell", None, None)),
        check_vma=False,
    )
```

```python
import functools

import jax
import jax.numpy as jnp
from jax import lax
from jax.experimental import pallas as pl
from jax.experimental.pallas import tpu as pltpu
from jax.sharding import PartitionSpec as P

TILE = 48
LANES = 128
LOG2E = 1.4426950408889634
MESH = pl.DeviceIdType.MESH
F32 = jnp.float32
BF16 = jnp.bfloat16


def split(value):
    high = value.astype(BF16)
    return high, (value - high.astype(F32)).astype(BF16)


def dot(left, right):
    return jnp.dot(left, right, preferred_element_type=F32)


def dot_nt(left, right):
    return lax.dot_general(left, right, (((1,), (1,)), ((), ())), preferred_element_type=F32)


def cell_peers(cells, me):
    side = me % 2
    base = me - side
    peers = [((base + 1 - side) % cells, 0, 3 - side, 2 + side)]
    for pair in (-1, 1):
        for other in (0, 1):
            cell = (base + 2 * pair + other + cells) % cells
            peers.append((cell, pair, 2 * pair + 2 + other, side + 2 - 2 * pair))
    return peers


def pair_ids(even, odd, slots):
    count = even[0:1, 0:1]
    ids = []
    for s in range(slots + 1):
        picked = even[0:1, 1 + min(s, slots - 1) : 2 + min(s, slots - 1)]
        for k in range(slots):
            picked = jnp.where(count == s - k, odd[0:1, 1 + k : 2 + k], picked)
        ids.append(picked)
    return ids


def over(value, divisor):
    return jnp.floor((value + 0.5) * (1.0 / divisor))


def iota(shape, axis):
    return lax.broadcasted_iota(jnp.int32, shape, axis).astype(F32)


def round_up(value, unit):
    return -(-value // unit) * unit


def step_kernel(
    cells, views, slots, rows, chunk, sub,
    count_ref, block_ref, ray_ref, shift_ref, gauss_in, tgt_in, out_ref, out_img,
    gauss_ref, gauss_parts, tgt_ref, tgts, info, infos, half_out, resp, got, par_ref, grad_ref, got_grad,
    img_out, img_in, part, quarter, full, alphas, weights, w_pair, stage, h_pair, moments, cgrads, flat_x, delta_x, cross_y, flat_y,
    load_sem, info_send, info_recv, tgt_send, tgt_recv, blk_send, blk_recv,
    img_send, img_recv, seg_send, seg_recv, part_send, part_recv, full_send, full_recv,
):
    me = lax.axis_index("cell")
    view = lax.axis_index("view")
    side = me % 2
    segs = slots + 1
    dense_rows, size = gauss_ref.shape
    per_block = dense_rows // rows
    pack = par_ref.shape[0]
    half = tgts.shape[2]
    channels = tgt_ref.shape[0]
    peers = cell_peers(cells, me)
    others = [(view + k) % views for k in range(1, views)]

    def to_cell(src, dst, send, recv, cell):
        return pltpu.make_async_remote_copy(
            src, dst, send, recv, device_id={"cell": cell}, device_id_type=MESH
        )

    def to_view(src, dst, send, recv, other):
        return pltpu.make_async_remote_copy(
            src, dst, send, recv, device_id={"view": other}, device_id_type=MESH
        )

    gauss_load = pltpu.make_async_copy(gauss_in, gauss_ref, load_sem.at[0])
    gauss_load.start()
    tgt_load = pltpu.make_async_copy(tgt_in, tgt_ref, load_sem.at[1])
    tgt_load.start()
    barrier = pltpu.get_barrier_semaphore()
    for cell, _, _, _ in peers:
        pl.semaphore_signal(barrier, inc=1, device_id={"cell": cell}, device_id_type=MESH)
    for other in others:
        pl.semaphore_signal(barrier, inc=1, device_id={"view": other}, device_id_type=MESH)
    lane = lax.broadcasted_iota(jnp.int32, info.shape, 1)
    fields = jnp.where(lane == 0, count_ref[0, 0], 0)
    for s in range(slots):
        fields = jnp.where(lane == 1 + s, block_ref[0, 0, s], fields)
    fields = jnp.where(lane == 1 + slots, ray_ref[0, 0], fields)
    info[...] = fields
    infos[2 + side] = fields
    gauss_load.wait()
    gauss = gauss_ref[...]
    high = gauss.astype(BF16)
    rest = gauss - high.astype(F32)
    middle = rest.astype(BF16)
    gauss_parts[:dense_rows] = high
    gauss_parts[dense_rows : 2 * dense_rows] = middle
    gauss_parts[2 * dense_rows : 3 * dense_rows] = (rest - middle.astype(F32)).astype(BF16)
    spare = gauss_parts.shape[0] - 3 * dense_rows
    if spare:
        gauss_parts[3 * dense_rows :] = jnp.zeros((spare, size), BF16)
    tgt_load.wait()
    blank = jnp.zeros((8 - channels, half), F32)

    def tile_half(which):
        cols = pl.ds(pl.multiple_of(which * half, LANES), half)
        return jnp.concatenate([tgt_ref[r, :, cols] for r in range(channels)] + [blank], axis=0)

    half_out[...] = tile_half(1 - side)
    tgts[side] = tile_half(side)
    moments[...] = jnp.zeros_like(moments)
    cgrads[...] = jnp.zeros_like(cgrads)
    pl.semaphore_wait(barrier, len(peers) + len(others))

    sends = []
    for n, (cell, _, _, theirs) in reversed(list(enumerate(peers))):
        sends.append(to_cell(info, infos.at[theirs], info_send.at[n], info_recv.at[theirs], cell))
        sends[-1].start()
    tgt_copy = to_cell(half_out, tgts.at[side], tgt_send, tgt_recv, peers[0][0])
    tgt_copy.start()

    row_id = iota((pack, gauss_parts.shape[0]), 0)
    row_param = over(row_id, segs)
    row_slot = row_id - segs * row_param
    lane_id = iota((pack, gauss_parts.shape[0]), 1)
    lane_part = over(lane_id, dense_rows)
    lane_id = lane_id - dense_rows * lane_part
    lane_param = over(lane_id, per_block)
    same = (row_param == lane_param) & (lane_part < 3.0)
    lane_block = lane_id - per_block * lane_param
    local = {}
    for pair in (-1, 1, 0):
        for n, (cell, distance, mine, _) in enumerate(peers):
            if distance == pair:
                to_cell(info, infos.at[mine], info_send.at[n], info_recv.at[mine], cell).wait_recv()
        ids = pair_ids(infos[2 * pair + 2], infos[2 * pair + 3], slots)
        local[pair] = [(block - me * per_block).astype(F32) for block in ids]
        wanted = jnp.full(row_id.shape, -1.0, F32)
        for s in range(segs):
            wanted = jnp.where(row_slot == float(s), local[pair][s], wanted)
        chosen = jnp.where(same & (lane_block == wanted), 1.0, 0.0).astype(BF16)
        resp[pair + 1] = dot(chosen, gauss_parts[...])
        for n, (cell, distance, _, theirs) in enumerate(peers):
            if distance == pair:
                sends.append(to_cell(resp.at[pair + 1], got.at[theirs], blk_send.at[n], blk_recv.at[theirs], cell))
                sends[-1].start()

    even, odd = infos[2], infos[3]
    count, ray_even, ray_odd = even[0:1, 0:1], even[0:1, slots + 1 : slots + 2], odd[0:1, slots + 1 : slots + 2]
    shift_x, shift_y = shift_ref[0:1, 0:1], shift_ref[0:1, 1:2]
    centre = (TILE - 1) / 2.0
    row_ids = lax.broadcasted_iota(jnp.int32, (size, size), 0)
    col_ids = lax.broadcasted_iota(jnp.int32, (size, size), 1)
    before = (row_ids < col_ids).astype(F32).astype(BF16)
    after = (row_ids > col_ids).astype(F32).astype(BF16)
    before = jnp.concatenate([before, before], axis=0)
    after = jnp.concatenate([after, after], axis=0)
    parts = [slice(r, r + sub) for r in range(0, chunk, sub)]
    whole = slice(0, chunk)
    dense_row = iota((dense_rows, round_up(3 * pack, LANES)), 0)
    dense_param = over(dense_row, per_block)
    dense_block = dense_row - per_block * dense_param
    pack_lane = iota(dense_row.shape, 1)
    pack_pair = over(pack_lane, pack)
    pack_lane = pack_lane - pack * pack_pair
    pack_param = over(pack_lane, segs)
    pack_slot = pack_lane - segs * pack_param
    wanted = jnp.full(dense_row.shape, -1.0, F32)
    for pair in (-1, 0, 1):
        for s in range(segs):
            here = (pack_pair == float(pair + 1)) & (pack_slot == float(s))
            wanted = jnp.where(here, local[pair][s], wanted)
    placing = jnp.where((dense_param == pack_param) & (dense_block == wanted), 1.0, 0.0).astype(BF16)

    total = resp[1]
    for n, (cell, distance, mine, _) in enumerate(peers):
        to_cell(resp.at[distance + 1], got.at[mine], blk_send.at[n], blk_recv.at[mine], cell).wait_recv()
        total = total + got[mine]
    par_ref[...] = total
    tgt_copy.wait_recv()

    def param(s, r):
        return par_ref[r * segs + s : r * segs + s + 1]

    def place(ids):
        ids = ids.astype(F32)
        row = over(ids, TILE)
        return ids - TILE * row - centre, row - centre

    def at(s, rows):
        return slice(s * chunk + rows.start, s * chunk + rows.stop)

    image_rows, shade_rows = [], []
    for s in range(segs):
        colours = jnp.concatenate([param(s, 6 + r) for r in range(3)] + [jnp.zeros((5, size), F32)], axis=0)
        in_even = (count > s).astype(F32)
        both = jnp.concatenate([colours * in_even, colours * (1.0 - in_even)], axis=0)
        c_hi = both.astype(BF16).astype(F32)
        c_lo = both - c_hi
        pieces = jnp.concatenate([c_hi, c_lo], axis=0).astype(BF16)
        image_rows.append(jnp.concatenate([pieces, pieces], axis=1))
        shade_rows.append(
            jnp.concatenate([c_hi, c_hi, c_lo, jnp.zeros((LANES - 48, size), F32)], axis=0).astype(BF16)
        )
    shade_rows = jnp.concatenate(shade_rows, axis=1)
    x_0 = iota((TILE, size), 0) - centre - shift_x
    y_0 = iota(flat_y.shape[1:], 0) + (side * (half // TILE)).astype(F32) - centre - shift_y
    for s in range(segs):
        dx = x_0 - param(s, 0)
        dy = y_0 - param(s, 1)
        delta_x[s] = dx
        flat_x[s] = ((-0.5 * LOG2E) * param(s, 2)) * dx * dx + LOG2E * jnp.log(param(s, 5))
        cross_y[s] = (-LOG2E) * param(s, 3) * dy
        flat_y[s] = ((-0.5 * LOG2E) * param(s, 4)) * dy * dy

    def steps(c):
        cols = slice(c * chunk, (c + 1) * chunk)
        first = side * half + c * chunk
        for s in range(segs):
            for k in range(chunk // TILE):
                rows = slice(k * TILE, (k + 1) * TILE)
                r = c * (chunk // TILE) + k
                power = flat_x[s] + delta_x[s] * cross_y[s, r : r + 1] + flat_y[s, r : r + 1]
                alpha = jnp.exp2(power)
                alphas[c, at(s, rows)] = alpha
                high, low = split(jnp.log(1.0 - alpha))
                stage[c, at(s, rows), :size] = high
                stage[c, at(s, rows), size:] = low
        yield
        prefix = dot(stage[c], before)
        yield
        for rows in parts:
            carry = jnp.ones((sub, 1), F32)
            for s in range(segs):
                alpha = alphas[c, at(s, rows)]
                trans = jnp.exp(prefix[at(s, rows)]) * carry
                weight = alpha * trans
                weights[c, at(s, rows)] = weight
                high, low = split(weight)
                w_pair[c, at(s, rows), :size] = high
                w_pair[c, at(s, rows), size:] = low
                carry = jnp.where(count == s + 1, 1.0, (trans - weight)[:, size - 1 :])
        yield
        image = jnp.zeros((32, chunk), F32)
        for s in range(segs):
            image = image + dot_nt(image_rows[s], w_pair[c, at(s, whole)])
        yield
        in_tile = lax.broadcasted_iota(jnp.int32, (16, chunk), 0) < 8
        lane_ids = first + lax.broadcasted_iota(jnp.int32, (16, chunk), 1)
        live = (lane_ids < jnp.where(in_tile, ray_even, ray_odd)).astype(F32)
        rendered = (image[:16] + image[16:]) * live
        own = jnp.where(side == 0, rendered[:8], rendered[8:])
        img_out[:, cols] = jnp.where(side == 0, rendered[8:], rendered[:8])
        for r in range(channels):
            out_img[r, :, pl.ds(pl.multiple_of(first, LANES), chunk)] = own[r : r + 1]
        target = jnp.concatenate([tgts[0, :, cols], tgts[1, :, cols]], axis=0)
        residual = (rendered - target) * live
        r_hi = residual.astype(BF16).astype(F32)
        r_lo = residual - r_hi
        spread = jnp.concatenate([r_hi, r_lo, r_hi, jnp.zeros((LANES - 48, chunk), F32)], axis=0)
        spread = jnp.transpose(spread).astype(BF16)
        r_rows = jnp.concatenate([r_hi, r_lo], axis=0).astype(BF16)
        x_l, y_l = place(lane_ids[:1])
        squares = [x_l * x_l, x_l * y_l, y_l * y_l]
        sq_hi = [q.astype(BF16).astype(F32) for q in squares]
        none = jnp.zeros_like(x_l)
        features = [none + 1.0, x_l, y_l] + sq_hi + [none] * 5 + [q - h for q, h in zip(squares, sq_hi)] + [none] * 2
        features = jnp.concatenate(features, axis=0).astype(BF16)
        features = jnp.concatenate([features, features], axis=1)
        shaded = dot(spread, shade_rows)
        yield
        for rows in parts:
            for s in range(segs):
                product = weights[c, at(s, rows)] * shaded[rows, s * size : (s + 1) * size]
                weights[c, at(s, rows)] = product
                high, low = split(product)
                stage[c, at(s, rows), :size] = high
                stage[c, at(s, rows), size:] = low
        yield
        later = dot(stage[c], after)
        for s in range(segs):
            cgrads[s] += dot(r_rows, w_pair[c, at(s, whole)])
        yield
        for rows in parts:
            carry = jnp.zeros((sub, 1), F32)
            for s in reversed(range(segs)):
                product = weights[c, at(s, rows)]
                alpha = alphas[c, at(s, rows)]
                tail = later[at(s, rows)] + carry
                carry = jnp.where(count == s, 0.0, (tail + product)[:, :1])
                rest = 1.0 - alpha
                inverse = pl.reciprocal(rest, approx=True)
                inverse = inverse * (2.0 - rest * inverse)
                high, low = split(product - alpha * inverse * tail)
                h_pair[c, s, rows] = high
                h_pair[c, s, slice(chunk + rows.start, chunk + rows.stop)] = low
        yield
        for s in range(segs):
            moments[s] += dot(features, h_pair[c, s])
        yield

    chunks = [steps(c) for c in range(half // chunk)]
    for tick in range(9 + len(chunks) - 1):
        for c, stages in enumerate(chunks):
            if 0 <= tick - c < 9:
                next(stages)

    img_copy = to_cell(img_out, img_in, img_send, img_recv, peers[0][0])
    img_copy.start()
    grad_ref[...] = jnp.zeros_like(grad_ref)
    for s in range(segs):
        row = functools.partial(param, s)
        mean_x, mean_y = row(0) + shift_x, row(1) + shift_y
        m = [moments[s, k : k + 1] for k in range(3)] + [
            moments[s, k : k + 1] + moments[s, k + 8 : k + 9] for k in range(3, 6)
        ]
        along_x = m[1] - mean_x * m[0]
        along_y = m[2] - mean_y * m[0]
        square_x = m[3] - 2.0 * mean_x * m[1] + mean_x * mean_x * m[0]
        cross_xy = m[4] - mean_x * m[2] - mean_y * m[1] + mean_x * mean_y * m[0]
        square_y = m[5] - 2.0 * mean_y * m[2] + mean_y * mean_y * m[0]
        cg = cgrads[s, :16] + cgrads[s, 16:]
        cg = cg[:, :size] + cg[:, size:]
        grads = [
            row(2) * along_x + row(3) * along_y,
            row(3) * along_x + row(4) * along_y,
            -0.5 * square_x,
            -cross_xy,
            -0.5 * square_y,
            m[0] / row(5),
            jnp.where(count > s, cg[0:3], cg[8:11]),
        ]
        for r, value in enumerate(grads[:6] + [grads[6][k : k + 1] for k in range(3)]):
            grad_ref[r * segs + s : r * segs + s + 1] = value

    for n, (cell, _, _, theirs) in reversed(list(enumerate(peers))):
        sends.append(to_cell(grad_ref, got_grad.at[theirs], seg_send.at[n], seg_recv.at[theirs], cell))
        sends[-1].start()
    sums = {}
    for pair in (0, -1, 1):
        for n, (cell, distance, mine, _) in enumerate(peers):
            if distance == pair:
                to_cell(grad_ref, got_grad.at[mine], seg_send.at[n], seg_recv.at[mine], cell).wait_recv()
        if pair == 0:
            sums[pair] = grad_ref[...] + got_grad[3 - side]
        else:
            sums[pair] = got_grad[2 * pair + 2] + got_grad[2 * pair + 3]
    spare = placing.shape[1] - 3 * pack
    stacked = [sums[-1], sums[0], sums[1]] + ([jnp.zeros((spare, size), F32)] if spare else [])
    high, low = split(jnp.concatenate(stacked, axis=0))
    dense = dot(placing, high) + dot(placing, low)
    part[:dense_rows] = dense[:, : size // 2]
    part[dense_rows:] = dense[:, size // 2 :]

    share = part.shape[0] // views

    def share_of(which):
        return pl.ds(pl.multiple_of(which * share, 8), share)

    part_copies = []
    for k, other in enumerate(others):
        part_copies.append(to_view(part.at[share_of(other)], quarter.at[k], part_send.at[k], part_recv.at[k], other))
        part_copies[-1].start()
    total = part[share_of(view)]
    for k, copy in enumerate(part_copies):
        copy.wait_recv()
        total = total + quarter[k]
    full[share_of(view)] = total
    for k, other in enumerate(others):
        mine = full.at[share_of(view)]
        sends.append(to_view(mine, mine, full_send.at[k], full_recv.at[k], other))
        sends[-1].start()
    img_copy.wait_recv()
    for r in range(channels):
        out_img[r, :, pl.ds(pl.multiple_of((1 - side) * half, LANES), half)] = img_in[r : r + 1]
    for k in range(views - 1):
        theirs = full.at[share_of((view + views - 1 - k) % views)]
        to_view(theirs, theirs, full_send.at[k], full_recv.at[k], others[k]).wait_recv()
    out_ref[:, : size // 2] = full[:dense_rows]
    out_ref[:, size // 2 :] = full[dense_rows:]
    for copy in sends + part_copies + [tgt_copy, img_copy]:
        copy.wait_send()


def step(cells, views, seg_count, seg_block, ray_count, shift, gaussians, target, rows):
    slots = seg_block.shape[2]
    segs = slots + 1
    dense_rows, size = gaussians.shape
    half = target.shape[2] // 2
    chunk = next(c for c in (384, half) if half % c == 0)
    count = half // chunk
    pack = (round_up(rows * segs, 8), size)
    share = 2 * dense_rows // views
    vmem = pl.BlockSpec(memory_space=pltpu.VMEM)
    smem = pl.BlockSpec(memory_space=pltpu.SMEM)
    hbm = pl.BlockSpec(memory_space=pl.ANY)
    dma = pltpu.SemaphoreType.DMA
    return pl.pallas_call(
        functools.partial(step_kernel, cells, views, slots, rows, chunk, chunk),
        out_shape=(
            jax.ShapeDtypeStruct(gaussians.shape, F32),
            jax.ShapeDtypeStruct(target.shape, F32),
        ),
        in_specs=[smem] * 3 + [vmem] + [hbm] * 2,
        out_specs=(vmem,) * 2,
        scratch_shapes=[
            pltpu.VMEM(gaussians.shape, F32),
            pltpu.VMEM((round_up(3 * dense_rows, LANES), size), BF16),
            pltpu.VMEM(target.shape, F32),
            pltpu.VMEM((2, 8, half), F32),
            pltpu.VMEM((8, LANES), jnp.int32),
            pltpu.VMEM((6, 8, LANES), jnp.int32),
            pltpu.VMEM((8, half), F32),
            pltpu.VMEM((3,) + pack, F32),
            pltpu.VMEM((6,) + pack, F32),
            pltpu.VMEM(pack, F32),
            pltpu.VMEM(pack, F32),
            pltpu.VMEM((6,) + pack, F32),
            pltpu.VMEM((8, half), F32),
            pltpu.VMEM((8, half), F32),
            pltpu.VMEM((2 * dense_rows, size // 2), F32),
            pltpu.VMEM((views - 1, share, size // 2), F32),
            pltpu.VMEM((2 * dense_rows, size // 2), F32),
            pltpu.VMEM((count, segs * chunk, size), F32),
            pltpu.VMEM((count, segs * chunk, size), F32),
            pltpu.VMEM((count, segs * chunk, 2 * size), BF16),
            pltpu.VMEM((count, segs * chunk, 2 * size), BF16),
            pltpu.VMEM((count, segs, 2 * chunk, size), BF16),
            pltpu.VMEM((segs, 16, size), F32),
            pltpu.VMEM((segs, 32, 2 * size), F32),
            pltpu.VMEM((segs, TILE, size), F32),
            pltpu.VMEM((segs, TILE, size), F32),
            pltpu.VMEM((segs, half // TILE, size), F32),
            pltpu.VMEM((segs, half // TILE, size), F32),
            dma((2,)), dma((5,)), dma((6,)), dma, dma, dma((5,)), dma((6,)),
            dma, dma, dma((5,)), dma((6,)),
            dma((views - 1,)), dma((views - 1,)), dma((views - 1,)), dma((views - 1,)),
        ],
        compiler_params=pltpu.CompilerParams(
            collective_id=0, has_side_effects=True, vmem_limit_bytes=44 * 2**20
        ),
        name="splat_step",
    )(seg_count, seg_block, ray_count, shift, gaussians, target)


def shards(cells, views, gaussians, seg_count, seg_block, ray_count, camera_shift, target):
    blocks, rows, size = gaussians.shape
    by_row = gaussians.transpose(1, 0, 2).reshape(rows * blocks, size)
    planes = target.reshape(target.shape[2], 1, target.shape[3])
    grads, image = step(cells, views, seg_count, seg_block, ray_count, camera_shift, by_row, planes, rows)
    return (image.reshape(target.shape), grads.reshape(rows, blocks, size).transpose(1, 0, 2))


def solution(mesh):
    placed = (
        P("cell", None, None),
        P("view", "cell"),
        P("view", "cell", None),
        P("view", "cell"),
        P("view", None),
        P("view", "cell", None, None),
    )
    return jax.shard_map(
        functools.partial(shards, mesh.shape["cell"], mesh.shape["view"]),
        mesh=mesh,
        in_specs=placed,
        out_specs=(P("view", "cell", None, None), P("cell", None, None)),
        check_vma=False,
    )
```
